256 devices in a mesh: role: 4 (over z_lo), tp: 64 (over z_hi, x, y, core).
Axes of the slice: x: 4, y: 4, z: 8 (z_hi: 2, z_lo: 4; z = z_hi * 4 + z_lo), core: 2. Of those that a mesh axis runs over, the one named last changes fastest.
Arguments:
- queries: bfloat16 [32, 16384], P('role'), may hold values from -35 to 35
- cache: bfloat16 [8, 65536, 512], P('role', 'tp'), may hold values from -9 to 9
- beam_sequence: int32 [32], P('role'), may hold values from 0 to 1
- ffn_input: bfloat16 [128, 7168], P('role', 'tp'), may hold values from -6 to 6
- expert_ids: int32 [128, 3], P('role'), may hold values from 0 to 7, all different within a row; in each aligned block of 32 rows (0 to 31, 32 to 63, ...) at most 16 rows name the same one
- route_weights: float32 [128, 3], P('role'), may hold values from 0.2 to 1
- gate_up: bfloat16 [8, 7168, 2, 5120], P('role', None, None, 'tp'), may hold values from -0.0625 to 0.0625
- down_proj: bfloat16 [8, 5120, 7168], P('role', 'tp'), may hold values from -0.078125 to 0.078125
Outputs:
- attention_out: bfloat16 [32, 16384], P('role', 'tp')
- ffn_out: bfloat16 [128, 7168], P('role', 'tp')
The draws below stay inside these ranges and needn't reach their ends.
Inputs may be any that keep to these rules, and one draw needn't show every extreme that they name: `expert_ids`: each row names 3 different experts. Within the 32 rows of one group (rows g * 32 to (g + 1) * 32 - 1), no expert is named by more than 16 rows, and in some groups one expert is named by exactly 16.
All inputs are finite; a program needn't handle non-finite values.
Results may differ from the reference program's by a relative error of at most 0.013.
Values may be sent and summed in bfloat16 or wider, within the bound.
No kernel may reach another device: no remote copies, remote signals or barrier semaphores. Data moves between devices by JAX's collectives and lax.ppermute only.
A program may use at most 128 MiB of HBM per device.

```python
import math
import jax
import jax.numpy as jnp
import numpy as np
from jax import lax

D = 7168
FF = 5120
H = 64
HD = 256
ROWS_AG = 8
SEQ_G = 2
ROWS_BG = 32
TOPK = 3
CAP = 16
CTX = 65536
SEQS = 8
ROWS_A = 32
ROWS_B = 128
EXPERTS = 8


def draw_cache(key, part):
    key = jax.random.fold_in(key, 5)
    base = jnp.clip(jax.random.normal(key, (SEQS, CTX, 2 * HD), jnp.float32), -5.0, 5.0)
    return base.astype(jnp.bfloat16)


def draw_queries(key, part):
    key = jax.random.fold_in(key, 9)
    base = jnp.clip(jax.random.normal(key, (ROWS_A, H * HD), jnp.float32), -5.0, 5.0)
    return base.astype(jnp.bfloat16)


def place_ends(result, key, least, top_value):
    longest = result.shape.index(max(result.shape))
    spots = []
    for shift in (0, 1):
        where = [jax.random.randint(jax.random.fold_in(key, axis), (), 0, length) for axis, length in enumerate(result.shape)]
        where[longest] = (where[longest] + shift) % result.shape[longest]
        spots.append(tuple(where))
    return result.at[spots[0]].set(least).at[spots[1]].set(top_value)


def block_levels(own_key, dims, cuts, smallest, high):
    factor_of, own = 1.0, jax.random.fold_in(own_key, 6)
    for dim, parts in cuts:
        heights = jnp.exp(jax.random.uniform(jax.random.fold_in(own, dim), (parts,), jnp.float32, smallest / len(cuts), high / len(cuts)))
        factor_of = factor_of * jnp.repeat(heights, dims[dim] // parts).reshape([-1 if axis == dim else 1 for axis in range(len(dims))])
    return factor_of


def deal_out(rng, own, number, rows, count, top, bound, slope):
    ranking = jax.random.permutation(rng, count)
    heavy_load, common = shares(count, rows * top, bound, slope, True), shares(count, rows * top, bound, slope, False)
    places = jnp.arange(count)

    def named(tallies, turn):
        used = int((tallies > 0).sum())
        fixed = max(1, used // 4)
        moved = fixed + (places - fixed + turn * (used - fixed)) % max(1, count - fixed)
        return jnp.zeros((count,), jnp.int32).at[ranking[jnp.where(places < fixed, places, moved)]].set(jnp.asarray(tallies, jnp.int32))

    tallies = jnp.where(number % 4 == 0, named(heavy_load, number // 4), named(common, number - number // 4 - 1))
    mixed = jax.random.permutation(jax.random.fold_in(own, 3), count)
    source_of, sink = mixed[0:count // 2 * 2:2], mixed[1:count // 2 * 2:2]
    room = jnp.minimum(tallies[source_of] - 1, bound - tallies[sink]) // 2
    room = jnp.where((source_of == ranking[0]) | (sink == ranking[0]) | (tallies[sink] == 0), 0, jnp.maximum(room, 0))
    moved = jax.random.randint(jax.random.fold_in(own, 4), (count // 2,), 0, 1 << 20) % (room + 1)
    tallies = tallies.at[source_of].add(-moved).at[sink].add(moved)
    labels = jnp.searchsorted(jnp.cumsum(tallies), jnp.arange(rows * top), side="right").astype(jnp.int32)
    listing = labels.reshape(top, rows).T
    listing = listing[jax.random.permutation(jax.random.fold_in(own, 1), rows)]
    turn = jax.random.randint(jax.random.fold_in(own, 2), (rows, 1), 0, top)
    return jnp.take_along_axis(listing, (jnp.arange(top)[None, :] + turn) % top, axis=1)


def shares(count, total, reach, lean, full):
    loads = [(1 << 20) // math.isqrt(grade ** lean) + 1 for grade in range(1, count + 1)]
    largest = reach if full else min(reach, max(-(-total // count), total * loads[0] // sum(loads)))
    least = 1 if total - largest >= count - 1 else 0
    holding, rest = [largest] + [least] * (count - 1), total - largest - least * (count - 1)
    while rest > 0:
        free = [i for i in range(1, count) if holding[i] < largest] or [i for i in range(1, count) if holding[i] < reach]
        whole, left = sum([loads[i] for i in free]), rest
        for i in free:
            extra = min(reach - holding[i], max(1, left * loads[i] // whole), rest)
            holding[i] = holding[i] + extra
            rest = rest - extra
    return np.array(holding)


def gaussian(own_key, extent, width, bound, cuts=(), kind=jnp.bfloat16):
    entries = width * jax.random.normal(own_key, extent, jnp.float32)
    if cuts:
        entries = entries * block_levels(own_key, extent, cuts, -0.22, 0.18)
    return jnp.clip(entries, -bound, bound).astype(kind)


def setup_inputs(seed: int = 0) -> dict:
    arg_keys = jax.random.split(jax.random.key(seed), 9)
    queries = draw_queries(jax.random.fold_in(arg_keys[8], 71), 0)
    cache = draw_cache(jax.random.fold_in(arg_keys[8], 71), 0)
    beam_sequence = place_ends(jax.random.randint(arg_keys[2], (ROWS_A,), 0, SEQ_G), jax.random.fold_in(arg_keys[2], 1), 0, SEQ_G - 1).astype(jnp.int32)
    ffn_input = gaussian(arg_keys[3], (ROWS_B, D), 1.0, 6.0, ((0, 4), (1, 64)))
    expert_ids_keys = jax.random.split(jax.random.fold_in(arg_keys[4], 1), ROWS_B // ROWS_BG)
    expert_ids_turns = jax.random.permutation(jax.random.fold_in(arg_keys[4], 3), ROWS_B // ROWS_BG)
    expert_ids = jax.vmap(lambda own, number: deal_out(jax.random.fold_in(arg_keys[4], 2), own, number, ROWS_BG, EXPERTS, TOPK, CAP, 2))(expert_ids_keys, expert_ids_turns).reshape((ROWS_B, TOPK))
    route_weights = jnp.clip(0.2 + 0.8 * jax.random.uniform(arg_keys[5], (ROWS_B, TOPK), jnp.float32) ** block_levels(arg_keys[5], (ROWS_B, TOPK), ((0, 4),), -0.2, 0.2), 0.2, 1.0)
    gate_up = gaussian(arg_keys[6], (EXPERTS, D, 2, FF), D ** -0.5, 0.0625, ((0, 4), (3, 64)))
    down_proj = gaussian(arg_keys[7], (EXPERTS, FF, D), FF ** -0.5, 0.078125, ((0, 4), (1, 64)))
    return dict(queries=queries, cache=cache, beam_sequence=beam_sequence, ffn_input=ffn_input, expert_ids=expert_ids, route_weights=route_weights, gate_up=gate_up, down_proj=down_proj)


def attend_row(item, cache):
    q_row, seq = item
    block = lax.dynamic_index_in_dim(cache, seq, 0, keepdims=False).astype(jnp.float32)
    query = q_row.reshape(H, HD).astype(jnp.float32)
    scores = jnp.einsum("hd,kd->hk", query, block[:, :HD]) * (HD ** -0.5)
    top = jnp.max(scores, axis=1, keepdims=True)
    expo = jnp.exp(scores - top)
    total = jnp.sum(expo, axis=1)
    rounded = lax.optimization_barrier(expo.astype(jnp.bfloat16)).astype(jnp.float32)
    summed = jnp.einsum("hk,kd->hd", rounded, block[:, HD:])
    return (summed / total[:, None]).reshape(-1).astype(jnp.bfloat16)


def reference(queries, cache, beam_sequence, ffn_input, expert_ids, route_weights, gate_up, down_proj):
    groups = jnp.arange(ROWS_A, dtype=jnp.int32) // ROWS_AG
    seq_index = (groups * SEQ_G + beam_sequence).astype(jnp.int32)
    attention_out = lax.map(lambda item: attend_row(item, cache), (queries, seq_index))

    def expert_apply(index):
        weight_pair = lax.dynamic_index_in_dim(gate_up, index, 0, keepdims=False)
        weight_down = lax.dynamic_index_in_dim(down_proj, index, 0, keepdims=False)
        gate = jnp.dot(ffn_input, weight_pair[:, 0, :], preferred_element_type=jnp.float32)
        upper = jnp.dot(ffn_input, weight_pair[:, 1, :], preferred_element_type=jnp.float32)
        hidden = (jax.nn.silu(gate) * upper).astype(jnp.bfloat16)
        return jnp.dot(hidden, weight_down, preferred_element_type=jnp.float32).astype(jnp.bfloat16)

    outputs = lax.map(expert_apply, jnp.arange(EXPERTS, dtype=jnp.int32))
    row_index = jnp.arange(ROWS_B, dtype=jnp.int32)[:, None]
    picked = outputs[expert_ids, row_index].astype(jnp.float32)
    ffn_out = jnp.sum(route_weights[:, :, None] * picked, axis=1).astype(jnp.bfloat16)
    return attention_out, ffn_out
```

```python
import jax
import jax.numpy as jnp
from jax import lax
from jax.experimental import pallas as pl
from jax.experimental.pallas import tpu as pltpu
from jax.sharding import Mesh
from jax.sharding import PartitionSpec as P

F32, BF16 = jnp.float32, jnp.bfloat16
VMEM = pl.BlockSpec(memory_space=pltpu.VMEM)
SMEM = pl.BlockSpec(memory_space=pltpu.SMEM)
XY = 16
BLK = 112
ROWS = 128
NX = 2 * BLK
NA = 48


def call(kernel, out_shape, args, specs=None, limit=16 << 20):
    many = isinstance(out_shape, (list, tuple))
    return pl.pallas_call(
        kernel,
        out_shape=out_shape,
        in_specs=specs or [VMEM] * len(args),
        out_specs=[VMEM] * len(out_shape) if many else VMEM,
        compiler_params=pltpu.CompilerParams(vmem_limit_bytes=limit),
    )(*args)


def split3(v):
    hi = v.astype(BF16).astype(F32)
    mid = (v - hi).astype(BF16).astype(F32)
    return hi, mid, (v - hi) - mid


def with_lse(out, lse):
    hi, mid, lo = split3(lse)
    lane = lax.broadcasted_iota(jnp.int32, (out.shape[0], 128), 1)
    tail = jnp.where(lane == 0, hi, jnp.where(lane == 1, mid, jnp.where(lane == 2, lo, 0.0)))
    return jnp.concatenate([out, tail], axis=1)


def lse_of(part):
    return jnp.sum(part[..., 256:], axis=-1, keepdims=True)


def attend_kernel(q_ref, cache_ref, pick_ref, out_ref):
    rows = q_ref.shape[0] * q_ref.shape[1]
    query = q_ref[...].astype(F32).reshape(rows, 256).astype(BF16)
    second = pick_ref[...] == 1
    dims = (((1,), (1,)), ((), ()))
    first_s = lax.dot_general(query, cache_ref[0, :, :256], dims, preferred_element_type=F32)
    second_s = lax.dot_general(query, cache_ref[1, :, :256], dims, preferred_element_type=F32)
    scores = jnp.where(second, second_s, first_s) * (256 ** -0.5)
    top = jnp.max(scores, axis=1, keepdims=True)
    expo = jnp.exp(scores - top)
    total = jnp.sum(expo, axis=1, keepdims=True)
    summed = jnp.dot(
        jnp.where(second, 0.0, expo).astype(BF16), cache_ref[0, :, 256:], preferred_element_type=F32
    ) + jnp.dot(
        jnp.where(second, expo, 0.0).astype(BF16), cache_ref[1, :, 256:], preferred_element_type=F32
    )
    both = with_lse(summed / total, top + jnp.log(total))
    out_ref[...] = both.reshape(out_ref.shape).astype(BF16)


def attend(queries, cache, beam_sequence):
    rows, heads = queries.shape[0], queries.shape[1] // 256
    chunk = 16
    query = queries.reshape(rows, heads, 256).transpose(1, 0, 2)
    pick = jnp.tile(beam_sequence, chunk)[:, None]
    return pl.pallas_call(
        attend_kernel,
        grid=(heads // chunk,),
        out_shape=jax.ShapeDtypeStruct((heads, rows, 384), BF16),
        in_specs=[
            pl.BlockSpec((chunk, rows, 256), lambda i: (i, 0, 0)),
            pl.BlockSpec(cache.shape, lambda i: (0, 0, 0)),
            pl.BlockSpec((chunk * rows, 1), lambda i: (0, 0)),
        ],
        out_specs=pl.BlockSpec((chunk, rows, 384), lambda i: (i, 0, 0)),
        compiler_params=pltpu.CompilerParams(vmem_limit_bytes=20 << 20),
    )(query, cache, pick)


def pair(first, second):
    lse_a, lse_b = lse_of(first), lse_of(second)
    top = jnp.maximum(lse_a, lse_b)
    wa, wb = jnp.exp(lse_a - top), jnp.exp(lse_b - top)
    total = wa + wb
    out = (first[..., :256] * wa + second[..., :256] * wb) / total
    return out, top + jnp.log(total)


def pack_kernel(index_ref, rows_ref, mine_ref, theirs_ref, out_ref, weight_ref):
    out, lse = pair(
        mine_ref[...].astype(F32).reshape(256, 384), theirs_ref[...].astype(F32).reshape(256, 384)
    )
    both = with_lse(out, lse).reshape(2, XY, 8, 384)
    pieces = [both[z, :, :, p * 128 : (p + 1) * 128] for z in range(2) for p in range(3)]
    out_ref[:, NX:, :] = jnp.concatenate(pieces, axis=1).astype(BF16)
    for z in range(2):
        block = jnp.concatenate([rows_ref[2 * r + z] for r in range(4)], axis=0)
        turned = block.astype(F32).T
        if z == 0:
            weight_ref[...] = turned[BLK : BLK + 8] + turned[BLK + 8 :]
        features = turned[:BLK].astype(BF16)
        for p in range(XY):
            out_ref[p, z * BLK : (z + 1) * BLK, :] = features


def ffn_kernel(index_ref, mine_ref, theirs_ref, weight_ref, gate_ref, down_ref, keep_ref, give_ref, x_ref):
    role, core = index_ref[0], index_ref[1]
    for z in range(2):
        for p in range(XY):
            start = (z * XY + p) * 2 * BLK
            x_ref[pl.ds(pl.multiple_of(start + core * BLK, 16), BLK), :] = mine_ref[
                p, z * BLK : (z + 1) * BLK, :
            ]
            x_ref[pl.ds(pl.multiple_of(start + (1 - core) * BLK, 16), BLK), :] = theirs_ref[
                p, z * BLK : (z + 1) * BLK, :
            ]
    units = gate_ref.shape[2]
    both = jnp.dot(
        gate_ref[...].reshape(4 * units, gate_ref.shape[3]), x_ref[...], preferred_element_type=F32
    )
    hidden = []
    for e in range(2):
        gate = both[2 * e * units : (2 * e + 1) * units]
        upper = both[(2 * e + 1) * units : (2 * e + 2) * units]
        weight = weight_ref[pl.ds(2 * role + e, 1), :]
        hidden.append(((gate / (1.0 + jnp.exp(-gate))) * upper * weight).astype(BF16))
    hidden = jnp.concatenate(hidden, axis=0)
    down = down_ref[...].reshape(2 * units, down_ref.shape[2])
    for z in range(2):
        for x in range(4):
            start = (z * 4 + x) * 8 * BLK
            part = lax.dot_general(
                down[:, start : start + 8 * BLK],
                hidden,
                (((0,), (0,)), ((), ())),
                preferred_element_type=F32,
            ).astype(BF16)
            for y in range(4):
                even = part[2 * y * BLK : (2 * y + 1) * BLK]
                odd = part[(2 * y + 1) * BLK : (2 * y + 2) * BLK]
                keep_ref[x * 4 + y, z * BLK : (z + 1) * BLK, :] = jnp.where(core == 0, even, odd)
                give_ref[x * 4 + y, z * BLK : (z + 1) * BLK, :] = jnp.where(core == 0, odd, even)


def add_kernel(a_ref, b_ref, out_ref):
    out_ref[...] = (a_ref[...].astype(F32) + b_ref[...].astype(F32)).astype(BF16)


def sum_kernel(parts_ref, out_ref):
    total = parts_ref[0].astype(F32)
    for p in range(1, XY):
        total += parts_ref[p].astype(F32)
    for z in range(2):
        turned = total[z * BLK : (z + 1) * BLK].T.astype(BF16)
        for r in range(4):
            out_ref[2 * r + z] = turned[32 * r : 32 * (r + 1)]


def last_kernel(parts_ref, out_ref):
    total = parts_ref[0].astype(F32)
    for p in range(1, 8):
        total += parts_ref[p].astype(F32)
    out_ref[...] = total.astype(BF16)


def merge_kernel(index_ref, parts_ref, mine_ref, theirs_ref):
    zhi = index_ref[2]
    parts = parts_ref[:, NX:, :].astype(F32)
    done = []
    for z in range(2):
        pieces = [parts[:, (z * 3 + p) * 8 : (z * 3 + p + 1) * 8, :] for p in range(3)]
        lse = jnp.sum(pieces[2], axis=-1, keepdims=True)
        top = jnp.max(lse, axis=0, keepdims=True)
        weight = jnp.exp(lse - top)
        total = jnp.sum(weight, axis=0)
        out = jnp.concatenate([jnp.sum(p * weight, axis=0) for p in pieces[:2]], axis=1) / total
        done.append(with_lse(out, top[0] + jnp.log(total)))
    mine_ref[...] = jnp.where(zhi == 0, done[0], done[1]).astype(BF16)
    theirs_ref[...] = jnp.where(zhi == 0, done[1], done[0]).astype(BF16)


def finish_kernel(a_ref, b_ref, out_ref):
    out, _ = pair(a_ref[...].astype(F32), b_ref[...].astype(F32))
    out_ref[...] = out.astype(BF16)


def shards(queries, cache, beam_sequence, ffn_input, expert_ids, route_weights, gate_up, down_proj):
    shape = jax.ShapeDtypeStruct
    swap = [(0, 1), (1, 0)]
    role, core, zhi = lax.axis_index("role"), lax.axis_index("core"), lax.axis_index("zhi")
    index = jnp.stack([role, core, zhi]).astype(jnp.int32)

    hits = expert_ids[:, :, None] == jnp.arange(8, dtype=jnp.int32)
    weights = jnp.sum(jnp.where(hits, route_weights[:, :, None], 0.0), axis=1)
    high = lax.reduce_precision(weights, 8, 7)
    low = weights - high
    message = jnp.concatenate([ffn_input, high.astype(BF16), low.astype(BF16)], axis=1)
    rows = lax.all_to_all(
        jnp.broadcast_to(message, (8, 32, 128)), ("role", "zhi"), 0, 0, tiled=True
    )

    attended = attend(queries, cache, beam_sequence).reshape(32, 2, 8, 384)
    mine = lax.dynamic_index_in_dim(attended, core, 1, False)
    theirs = lax.ppermute(lax.dynamic_index_in_dim(attended, 1 - core, 1, False), "core", swap)

    packed, weight = call(
        pack_kernel,
        [shape((XY, NX + NA, 128), BF16), shape((8, 128), F32)],
        (index, rows, mine, theirs),
        [SMEM, VMEM, VMEM, VMEM],
    )
    gathered = lax.all_to_all(packed, ("x", "y"), 0, 0, tiled=True)
    other = lax.ppermute(gathered, "core", swap)

    head, away = call(
        merge_kernel, [shape((8, 384), BF16)] * 2, (index, gathered), [SMEM, VMEM]
    )
    attention_out = call(
        finish_kernel, shape((8, 256), BF16), (head, lax.ppermute(away, "zhi", swap))
    )

    units = gate_up.shape[3]
    keep, give = pl.pallas_call(
        ffn_kernel,
        out_shape=[shape((XY, NX, 128), BF16)] * 2,
        in_specs=[SMEM] + [VMEM] * 5,
        out_specs=[VMEM] * 2,
        scratch_shapes=[pltpu.VMEM((64 * BLK, ROWS), BF16)],
        compiler_params=pltpu.CompilerParams(vmem_limit_bytes=24 << 20),
    )(index, gathered, other, weight, gate_up.transpose(0, 2, 3, 1), down_proj)
    half = call(add_kernel, shape((XY, NX, 128), BF16), (keep, lax.ppermute(give, "core", swap)))
    spread = lax.all_to_all(half, ("x", "y"), 0, 0, tiled=True)
    partial = call(sum_kernel, shape((8, 32, BLK), BF16), (spread,))
    ends = lax.all_to_all(partial, ("role", "zhi"), 0, 0, tiled=True)
    ffn_out = call(last_kernel, shape((32, BLK), BF16), (ends,))
    return (attention_out, ffn_out)


def solution(mesh):
    fine = Mesh(mesh.devices.reshape(4, 2, 4, 4, 2), ("role", "zhi", "x", "y", "core"))
    tp = ("zhi", "x", "y", "core")
    return jax.shard_map(
        shards,
        mesh=fine,
        in_specs=(
            P("role", None),
            P("role", tp, None),
            P("role"),
            P("role", tp),
            P("role", None),
            P("role", None),
            P("role", None, None, tp),
            P("role", tp, None),
        ),
        out_specs=(P("role", tp), P("role", tp)),
        check_vma=False,
    )
```

```python
import jax
import jax.numpy as jnp
from jax import lax
from jax.experimental import pallas as pl
from jax.experimental.pallas import tpu as pltpu
from jax.sharding import Mesh
from jax.sharding import PartitionSpec as P

F32, BF16 = jnp.float32, jnp.bfloat16
VMEM = pl.BlockSpec(memory_space=pltpu.VMEM)
SMEM = pl.BlockSpec(memory_space=pltpu.SMEM)
ANY = pl.BlockSpec(memory_space=pl.ANY)
HBM = pl.BlockSpec(memory_space=pltpu.HBM)
FULL = 62 << 20
XY = 16
BLK = 112
ROWS = 128
NX = 2 * BLK
NA = 48


def call(kernel, out_shape, args, specs=None, limit=16 << 20, scratch=(), cost=None, outs=None):
    many = isinstance(out_shape, (list, tuple))
    return pl.pallas_call(
        kernel,
        out_shape=out_shape,
        in_specs=specs or [VMEM] * len(args),
        out_specs=outs or ([VMEM] * len(out_shape) if many else VMEM),
        scratch_shapes=scratch,
        cost_estimate=cost,
        compiler_params=pltpu.CompilerParams(vmem_limit_bytes=limit),
    )(*args)


def split3(v):
    hi = v.astype(BF16).astype(F32)
    mid = (v - hi).astype(BF16).astype(F32)
    return hi, mid, (v - hi) - mid


def with_lse(out, lse):
    hi, mid, lo = split3(lse)
    lane = lax.broadcasted_iota(jnp.int32, (out.shape[0], 128), 1)
    tail = jnp.where(lane == 0, hi, jnp.where(lane == 1, mid, jnp.where(lane == 2, lo, 0.0)))
    return jnp.concatenate([out, tail], axis=1)


def lse_of(part):
    return jnp.sum(part[..., 256:], axis=-1, keepdims=True)


def prep_kernel(x_hbm, ids_hbm, route_hbm, out_ref, rows_ref, ids_ref, route_ref, turn_ref, sems):
    copies = [
        pltpu.make_async_copy(src, dst, sems.at[i])
        for i, (src, dst) in enumerate(((ids_hbm, ids_ref), (route_hbm, route_ref), (x_hbm, rows_ref)))
    ]
    for copy in copies:
        copy.start()
    turn_ref[...] = jnp.zeros_like(turn_ref)
    expert = lax.broadcasted_iota(jnp.int32, (8, 32), 0)
    weight = jnp.zeros((8, 32), F32)
    copies[0].wait()
    copies[1].wait()
    for k in range(3):
        weight += jnp.where(ids_ref[k : k + 1, :] == expert, route_ref[k : k + 1, :], 0.0)
    high = weight.astype(BF16).astype(F32)
    turn_ref[BLK : BLK + 8, :32] = high
    turn_ref[BLK + 8 :, :32] = weight - high
    turned = turn_ref[...].T[:32]
    copies[2].wait()
    wide = jnp.concatenate([rows_ref[...].astype(F32), jnp.zeros((32, 128 - BLK), F32)], axis=1)
    message = (wide + turned).astype(BF16)
    for p in range(8):
        out_ref[p] = message


def pack_kernel(rows_ref, out_ref, weight_ref):
    for z in range(2):
        block = jnp.concatenate([rows_ref[2 * r + z] for r in range(4)], axis=0)
        turned = block.astype(F32).T
        if z == 0:
            weight_ref[...] = turned[BLK : BLK + 8] + turned[BLK + 8 :]
        features = turned[:BLK].astype(BF16)
        for p in range(XY):
            out_ref[p, z * BLK : (z + 1) * BLK, :] = features


def attend(seq_ref, queries, caches, waits, out_ref):
    steps = len(queries)
    rows = queries[0].shape[0]
    place = lax.broadcasted_iota(jnp.int32, (rows, 1), 0) % 8
    pick = jnp.zeros((rows, 1), jnp.int32)
    for r in range(8):
        pick = jnp.where(place == r, seq_ref[r], pick)
    second = pick == 1
    dims = (((1,), (1,)), ((), ()))
    scores = [[] for _ in range(steps)]
    for k in range(2):
        waits[k]()
        for step in range(steps):
            both = [
                lax.dot_general(
                    queries[step], caches[k, s, :, :256], dims, preferred_element_type=F32
                )
                for s in range(2)
            ]
            scores[step].append(jnp.where(second, both[1], both[0]) * (256 ** -0.5))
    for step in range(steps):
        top = jnp.maximum(*(jnp.max(v, axis=1, keepdims=True) for v in scores[step]))
        total, summed = 0.0, 0.0
        for k in range(2):
            expo = jnp.exp(scores[step][k] - top)
            total += jnp.sum(expo, axis=1, keepdims=True)
            for s in range(2):
                part = jnp.where(second == (s == 1), expo, 0.0).astype(BF16)
                summed += jnp.dot(part, caches[k, s, :, 256:], preferred_element_type=F32)
        both = with_lse(summed / total, top + jnp.log(total)).reshape(rows // 8, 8, 384)
        out_ref[step * (rows // 8) : (step + 1) * (rows // 8)] = both.astype(BF16)


def local_kernel(
    seq_ref, q_hbm, mine_hbm, theirs_hbm, gate_hbm, got_gate_hbm, down_hbm, got_down_hbm, after_ref,
    attended_ref, out_g0_hbm, out_g1_hbm, out_d_ref,
    q_ref, cache_ref, in_ref, out_g_ref, cache_sems, in_sems, out_sems,
):
    core = lax.axis_index("core")
    units = in_ref.shape[1]
    positions = cache_ref.shape[2] // 4
    q_load = pltpu.make_async_copy(q_hbm.at[:, core], q_ref, cache_sems.at[16])
    q_load.start()
    cache_loads = []
    for k, ref in enumerate((mine_hbm, theirs_hbm)):
        for s in range(2):
            for i in range(4):
                at = (s, pl.ds(i * positions, positions))
                cache_loads.append(
                    pltpu.make_async_copy(
                        ref.at[at], cache_ref.at[(k,) + at], cache_sems.at[len(cache_loads)]
                    )
                )
                cache_loads[-1].start(priority=i % 2)
    sources = [ref.at[e, g] for ref in (gate_hbm, got_gate_hbm) for e in range(2) for g in range(2)]
    sources += [ref.at[e] for ref in (down_hbm, got_down_hbm) for e in range(2)]
    loads = [
        pltpu.make_async_copy(source, in_ref.at[i], in_sems.at[i]) for i, source in enumerate(sources)
    ]
    for i, load in enumerate(loads):
        load.start(priority=i % 2)

    def wait(k):
        for load in cache_loads[8 * k : 8 * k + 8]:
            load.wait()

    q_load.wait()
    queries = [
        q_ref[step * 16 : (step + 1) * 16].astype(F32).reshape(128, 256).astype(BF16)
        for step in range(2)
    ]
    attend(seq_ref, queries, cache_ref, [lambda: wait(0), lambda: wait(1)], attended_ref)

    stores = []
    for i in range(8):
        for piece in range(4):
            at = (piece, i // 4, pl.ds((i % 4) * units, units))
            to = (out_g0_hbm, out_g1_hbm)[piece // 2].at[(piece % 2,) + at[1:]]
            stores.append(
                pltpu.make_async_copy(out_g_ref.at[at], to, out_sems.at[len(stores)])
            )
    for i, load in enumerate(loads):
        load.wait()
        out = out_g_ref if i < 8 else out_d_ref
        k, row = (i // 4, (i % 4) * units) if i < 8 else ((i - 8) // 2, (i % 2) * units)
        for parity in range(2):

            @pl.when(core == parity)
            def _():
                for piece in range(4):
                    wide = [
                        in_ref[i, :, (z * 4 + piece) * 8 * BLK : (z * 4 + piece + 1) * 8 * BLK]
                        for z in range(2)
                    ]
                    parts = [
                        wide[z][:, (2 * p + parity) * BLK : (2 * p + parity + 1) * BLK]
                        for p in range(4)
                        for z in range(2)
                    ]
                    out[piece, k, row : row + units, :] = jnp.concatenate(parts, axis=1)

        for store in stores[4 * i : 4 * i + 4] if i < 8 else []:
            store.start()
    for store in stores:
        store.wait()


def up_first_kernel(rows_ref, gate_ref, out_ref):
    total = 0.0
    for piece in range(2):
        rows = rows_ref[4 * piece : 4 * piece + 4].reshape(8 * BLK, ROWS)
        total += jnp.dot(
            gate_ref[piece].reshape(-1, 8 * BLK), rows, preferred_element_type=F32
        )
    out_ref[...] = total.reshape(out_ref.shape)


def up_second_kernel(rows_ref, gate_ref, before_ref, out_ref):
    total = before_ref[...].reshape(-1, ROWS)
    for piece in range(2):
        rows = rows_ref[8 + 4 * piece : 12 + 4 * piece].reshape(8 * BLK, ROWS)
        total += jnp.dot(
            gate_ref[piece].reshape(-1, 8 * BLK), rows, preferred_element_type=F32
        )
    out_ref[...] = total.reshape(out_ref.shape)


def activate(both, weight_ref, role, units):
    hidden = []
    for e in range(2):
        gate = both[2 * e * units : (2 * e + 1) * units]
        upper = both[(2 * e + 1) * units : (2 * e + 2) * units]
        weight = weight_ref[pl.ds(2 * role + e, 1), :]
        hidden.append(((gate / (1.0 + jnp.exp(-gate))) * upper * weight).astype(BF16))
    return jnp.concatenate(hidden, axis=0)


def down_kernel(mine_ref, theirs_ref, weight_ref, down_ref, attended_ref, out_ref):
    role = lax.axis_index("role")
    units = mine_ref.shape[1] // 4
    hidden = [
        activate(mine_ref[k] + theirs_ref[1 - k], weight_ref, role, units) for k in range(2)
    ]
    dims = (((0,), (0,)), ((), ()))
    for piece in range(4):
        part = (
            lax.dot_general(down_ref[piece, 0], hidden[0], dims, preferred_element_type=F32)
            + lax.dot_general(down_ref[piece, 1], hidden[1], dims, preferred_element_type=F32)
        ).astype(BF16)
        out_ref[4 * piece : 4 * piece + 4, :NX, :] = part.reshape(4, NX, ROWS)
    both = attended_ref[...].astype(F32).reshape(2, XY, 8, 384)
    pieces = [both[z, :, :, p * 128 : (p + 1) * 128] for z in range(2) for p in range(3)]
    out_ref[:, NX:, :] = jnp.concatenate(pieces, axis=1).astype(BF16)


def turn_kernel(parts_ref, out_ref):
    total = parts_ref[0, :NX].astype(F32)
    for p in range(1, XY):
        total += parts_ref[p, :NX].astype(F32)
    parts = parts_ref[:, NX:, :].astype(F32)
    for z in range(2):
        pieces = [parts[:, (z * 3 + p) * 8 : (z * 3 + p + 1) * 8, :] for p in range(3)]
        lse = jnp.sum(pieces[2], axis=-1, keepdims=True)
        top = jnp.max(lse, axis=0, keepdims=True)
        weight = jnp.exp(lse - top)
        norm = jnp.sum(weight, axis=0)
        out = jnp.concatenate([jnp.sum(p * weight, axis=0) for p in pieces[:2]], axis=1) / norm
        head = with_lse(out, top[0] + jnp.log(norm))
        tail = [head[:, p * 128 : (p + 1) * 128] for p in range(3)] + [jnp.zeros((8, 128), F32)]
        tail = jnp.concatenate(tail, axis=0)
        turned = jnp.concatenate(
            [total[z * BLK : (z + 1) * BLK].T, jnp.zeros((ROWS, 128 - BLK), F32)], axis=1
        )
        for r in range(4):
            both = jnp.concatenate([turned[32 * r : 32 * (r + 1)], tail], axis=0)
            out_ref[2 * r + z] = both.astype(BF16)


def last_kernel(parts_ref, attention_ref, ffn_ref):
    total = parts_ref[0, :32].astype(F32)
    for p in range(1, 8):
        total += parts_ref[p, :32].astype(F32)
    ffn_ref[...] = total[:, :BLK].astype(BF16)
    role = lax.axis_index("role")
    heads = [parts_ref[2 * role + z, 32:].astype(F32) for z in range(2)]
    lse = [jnp.sum(h[16:24], axis=-1, keepdims=True) for h in heads]
    top = jnp.maximum(lse[0], lse[1])
    weight = [jnp.exp(v - top) for v in lse]
    out = [
        (heads[0][half] * weight[0] + heads[1][half] * weight[1]) / (weight[0] + weight[1])
        for half in (slice(0, 8), slice(8, 16))
    ]
    attention_ref[...] = jnp.concatenate(out, axis=1).astype(BF16)


def shards(queries, cache, beam_sequence, ffn_input, expert_ids, route_weights, gate_up, down_proj):
    shape = jax.ShapeDtypeStruct
    swap = [(0, 1), (1, 0)]

    message = call(
        prep_kernel,
        shape((8, 32, 128), BF16),
        (ffn_input, expert_ids.T, route_weights.T),
        [HBM] * 3,
        FULL,
        scratch=[
            pltpu.VMEM((32, BLK), BF16),
            pltpu.VMEM((3, 32), jnp.int32),
            pltpu.VMEM((3, 32), F32),
            pltpu.VMEM((128, 128), F32),
            pltpu.SemaphoreType.DMA((3,)),
        ],
    )
    rows = lax.all_to_all(message, ("role", "zhi"), 0, 0, tiled=True)
    packed, weight = call(pack_kernel, [shape((XY, NX, 128), BF16), shape((8, 128), F32)], (rows,))
    gathered = lax.all_to_all(packed, ("x", "y"), 0, 0, tiled=True)

    query = queries.reshape(8, 32, 2, 256).transpose(1, 2, 0, 3)
    gate = gate_up.transpose(0, 2, 3, 1)
    units = gate_up.shape[3]
    pairs = [w for a in (cache, gate, down_proj) for w in (a, lax.ppermute(a, "core", swap))]
    attended, gate_0, gate_1, down_c = call(
        local_kernel,
        [
            shape((32, 8, 384), BF16),
            shape((2, 2, 4 * units, 8 * BLK), BF16),
            shape((2, 2, 4 * units, 8 * BLK), BF16),
            shape((4, 2, 2 * units, 8 * BLK), BF16),
        ],
        (beam_sequence, query, *pairs, packed),
        [SMEM] + [HBM] * 7 + [ANY],
        FULL,
        [
            pltpu.VMEM((32, 8, 256), BF16),
            pltpu.VMEM((2,) + cache.shape, BF16),
            pltpu.VMEM((12, units, 64 * BLK), BF16),
            pltpu.VMEM((4, 2, 4 * units, 8 * BLK), BF16),
            pltpu.SemaphoreType.DMA((17,)),
            pltpu.SemaphoreType.DMA((12,)),
            pltpu.SemaphoreType.DMA((32,)),
        ],
        pl.CostEstimate(flops=1 << 31, bytes_accessed=24 << 20, transcendentals=1 << 19),
        [VMEM, HBM, HBM, VMEM],
    )

    first = shape((2, 4 * units, ROWS), F32)
    first = call(up_first_kernel, first, (gathered, gate_0))
    first = call(up_second_kernel, first, (gathered, gate_1, first))
    half = call(
        down_kernel,
        shape((XY, NX + NA, 128), BF16),
        (first, lax.ppermute(first, "core", swap), weight, down_c, attended),
    )
    spread = lax.all_to_all(half, ("x", "y"), 0, 0, tiled=True)
    partial = call(turn_kernel, shape((8, 64, 128), BF16), (spread,))
    ends = lax.all_to_all(partial, ("role", "zhi"), 0, 0, tiled=True)
    attention_out, ffn_out = call(
        last_kernel, [shape((8, 256), BF16), shape((32, BLK), BF16)], (ends,)
    )
    return (attention_out, ffn_out)


def solution(mesh):
    fine = Mesh(mesh.devices.reshape(4, 2, 4, 4, 2), ("role", "zhi", "x", "y", "core"))
    tp = ("zhi", "x", "y", "core")
    return jax.shard_map(
        shards,
        mesh=fine,
        in_specs=(
            P("role", None),
            P("role", tp, None),
            P("role"),
            P("role", tp),
            P("role", None),
            P("role", None),
            P("role", None, None, tp),
            P("role", tp, None),
        ),
        out_specs=(P("role", tp), P("role", tp)),
        check_vma=False,
    )
```

```python
import jax
import jax.numpy as jnp
from jax import lax
from jax.experimental import pallas as pl
from jax.experimental.pallas import tpu as pltpu
from jax.sharding import Mesh
from jax.sharding import PartitionSpec as P

F32, BF16 = jnp.float32, jnp.bfloat16
VMEM = pl.BlockSpec(memory_space=pltpu.VMEM)
SMEM = pl.BlockSpec(memory_space=pltpu.SMEM)
ANY = pl.BlockSpec(memory_space=pl.ANY)
HBM = pl.BlockSpec(memory_space=pltpu.HBM)
FULL = 62 << 20
XY = 16
BLK = 112
ROWS = 128
NX = 2 * BLK
NA = 48


def call(kernel, out_shape, args, specs=None, limit=16 << 20, scratch=(), cost=None, outs=None):
    many = isinstance(out_shape, (list, tuple))
    return pl.pallas_call(
        kernel,
        out_shape=out_shape,
        in_specs=specs or [VMEM] * len(args),
        out_specs=outs or ([VMEM] * len(out_shape) if many else VMEM),
        scratch_shapes=scratch,
        cost_estimate=cost,
        compiler_params=pltpu.CompilerParams(vmem_limit_bytes=limit),
    )(*args)


def split3(v):
    hi = v.astype(BF16).astype(F32)
    mid = (v - hi).astype(BF16).astype(F32)
    return hi, mid, (v - hi) - mid


def with_lse(out, lse):
    hi, mid, lo = split3(lse)
    lane = lax.broadcasted_iota(jnp.int32, (out.shape[0], 128), 1)
    tail = jnp.where(lane == 0, hi, jnp.where(lane == 1, mid, jnp.where(lane == 2, lo, 0.0)))
    return jnp.concatenate([out, tail], axis=1)


def lse_of(part):
    return jnp.sum(part[..., 256:], axis=-1, keepdims=True)


def prep_kernel(x_hbm, ids_hbm, route_hbm, out_ref, rows_ref, ids_ref, route_ref, turn_ref, sems):
    copies = [
        pltpu.make_async_copy(src, dst, sems.at[i])
        for i, (src, dst) in enumerate(((ids_hbm, ids_ref), (route_hbm, route_ref), (x_hbm, rows_ref)))
    ]
    for copy in copies:
        copy.start()
    turn_ref[...] = jnp.zeros_like(turn_ref)
    expert = lax.broadcasted_iota(jnp.int32, (8, 32), 0)
    weight = jnp.zeros((8, 32), F32)
    copies[0].wait()
    copies[1].wait()
    for k in range(3):
        weight += jnp.where(ids_ref[k : k + 1, :] == expert, route_ref[k : k + 1, :], 0.0)
    high = weight.astype(BF16).astype(F32)
    turn_ref[BLK : BLK + 8, :32] = high
    turn_ref[BLK + 8 :, :32] = weight - high
    turned = turn_ref[...].T[:32]
    copies[2].wait()
    wide = jnp.concatenate([rows_ref[...].astype(F32), jnp.zeros((32, 128 - BLK), F32)], axis=1)
    message = (wide + turned).astype(BF16)
    for p in range(8):
        out_ref[p] = message


def pack_kernel(rows_ref, out_ref, weight_ref):
    for z in range(2):
        block = jnp.concatenate([rows_ref[2 * r + z] for r in range(4)], axis=0)
        turned = block.astype(F32).T
        if z == 0:
            weight_ref[...] = turned[BLK : BLK + 8] + turned[BLK + 8 :]
        features = turned[:BLK].astype(BF16)
        for p in range(XY):
            out_ref[p, z * BLK : (z + 1) * BLK, :] = features


def attend(seq_ref, queries, caches, waits, out_ref):
    steps = len(queries)
    rows = queries[0].shape[0]
    place = lax.broadcasted_iota(jnp.int32, (rows, 1), 0) % 8
    pick = jnp.zeros((rows, 1), jnp.int32)
    for r in range(8):
        pick = jnp.where(place == r, seq_ref[r], pick)
    second = pick == 1
    dims = (((1,), (1,)), ((), ()))
    scores = [[] for _ in range(steps)]
    for k in range(2):
        waits[k]()
        for step in range(steps):
            both = [
                lax.dot_general(
                    queries[step], caches[k, s, :, :256], dims, preferred_element_type=F32
                )
                for s in range(2)
            ]
            scores[step].append(jnp.where(second, both[1], both[0]) * (256 ** -0.5))
    for step in range(steps):
        top = jnp.maximum(*(jnp.max(v, axis=1, keepdims=True) for v in scores[step]))
        total, summed = 0.0, 0.0
        for k in range(2):
            expo = jnp.exp(scores[step][k] - top)
            total += jnp.sum(expo, axis=1, keepdims=True)
            for s in range(2):
                part = jnp.where(second == (s == 1), expo, 0.0).astype(BF16)
                summed += jnp.dot(part, caches[k, s, :, 256:], preferred_element_type=F32)
        both = with_lse(summed / total, top + jnp.log(total)).reshape(rows // 8, 8, 384)
        out_ref[step * (rows // 8) : (step + 1) * (rows // 8)] = both.astype(BF16)


def local_kernel(
    seq_ref, q_hbm, mine_hbm, theirs_hbm, gate_hbm, got_gate_hbm, down_hbm, got_down_hbm, after_ref,
    attended_ref, out_g_hbm, out_d_ref,
    q_ref, cache_ref, in_ref, out_g_ref, cache_sems, in_sems, out_sems,
):
    core = lax.axis_index("core")
    units = in_ref.shape[1]
    positions = cache_ref.shape[2] // 4
    q_load = pltpu.make_async_copy(q_hbm.at[:, core], q_ref, cache_sems.at[16])
    q_load.start()
    cache_loads = []
    for k, ref in enumerate((mine_hbm, theirs_hbm)):
        for s in range(2):
            for i in range(4):
                at = (s, pl.ds(i * positions, positions))
                cache_loads.append(
                    pltpu.make_async_copy(
                        ref.at[at], cache_ref.at[(k,) + at], cache_sems.at[len(cache_loads)]
                    )
                )
                cache_loads[-1].start()
    sources = [ref.at[e, g] for ref in (gate_hbm, got_gate_hbm) for e in range(2) for g in range(2)]
    sources += [ref.at[e] for ref in (down_hbm, got_down_hbm) for e in range(2)]
    loads = [
        pltpu.make_async_copy(source, in_ref.at[i], in_sems.at[i]) for i, source in enumerate(sources)
    ]

    def wait(k):
        for load in cache_loads[8 * k : 8 * k + 8]:
            load.wait()
        if k == 1:
            for load in loads:
                load.start()

    q_load.wait()
    queries = [
        q_ref[step * 16 : (step + 1) * 16].astype(F32).reshape(128, 256).astype(BF16)
        for step in range(2)
    ]
    attend(seq_ref, queries, cache_ref, [lambda: wait(0), lambda: wait(1)], attended_ref)

    stores = []
    for i in range(8):
        at = (i // 4, pl.ds((i % 4) * units, units))
        stores.append(pltpu.make_async_copy(out_g_ref.at[at], out_g_hbm.at[at], out_sems.at[i]))
    for i, load in enumerate(loads):
        load.wait()
        out = out_g_ref if i < 8 else out_d_ref
        k, row = (i // 4, (i % 4) * units) if i < 8 else ((i - 8) // 2, (i % 2) * units)
        for parity in range(2):

            @pl.when(core == parity)
            def _():
                for piece in range(4):
                    wide = [
                        in_ref[i, :, (z * 4 + piece) * 8 * BLK : (z * 4 + piece + 1) * 8 * BLK]
                        for z in range(2)
                    ]
                    parts = [
                        wide[z][:, (2 * p + parity) * BLK : (2 * p + parity + 1) * BLK]
                        for p in range(4)
                        for z in range(2)
                    ]
                    to = slice(piece * 8 * BLK, (piece + 1) * 8 * BLK)
                    out[k, row : row + units, to] = jnp.concatenate(parts, axis=1)

        if i < 8:
            stores[i].start()
    for store in stores:
        store.wait()


def up_kernel(rows_ref, gate_ref, out_ref, send_ref):
    rows = rows_ref[...].reshape(XY * NX, ROWS)
    for k in range(2):
        both = jnp.dot(gate_ref[k], rows, preferred_element_type=F32)
        out_ref[k] = both
        send_ref[k] = both.astype(BF16)


def activate(both, weight_ref, role, units):
    hidden = []
    for e in range(2):
        gate = both[2 * e * units : (2 * e + 1) * units]
        upper = both[(2 * e + 1) * units : (2 * e + 2) * units]
        weight = weight_ref[pl.ds(2 * role + e, 1), :]
        hidden.append(((gate / (1.0 + jnp.exp(-gate))) * upper * weight).astype(BF16))
    return jnp.concatenate(hidden, axis=0)


def down_kernel(mine_ref, theirs_ref, weight_ref, down_ref, attended_ref, out_ref):
    role = lax.axis_index("role")
    units = mine_ref.shape[1] // 4
    hidden = [
        activate(mine_ref[k] + theirs_ref[1 - k].astype(F32), weight_ref, role, units) for k in range(2)
    ]
    dims = (((0,), (0,)), ((), ()))
    for piece in range(4):
        cut = slice(piece * 8 * BLK, (piece + 1) * 8 * BLK)
        part = (
            lax.dot_general(down_ref[0, :, cut], hidden[0], dims, preferred_element_type=F32)
            + lax.dot_general(down_ref[1, :, cut], hidden[1], dims, preferred_element_type=F32)
        ).astype(BF16)
        out_ref[4 * piece : 4 * piece + 4, :NX, :] = part.reshape(4, NX, ROWS)
    both = attended_ref[...].astype(F32).reshape(2, XY, 8, 384)
    pieces = [both[z, :, :, p * 128 : (p + 1) * 128] for z in range(2) for p in range(3)]
    out_ref[:, NX:, :] = jnp.concatenate(pieces, axis=1).astype(BF16)


def turn_kernel(parts_ref, out_ref):
    total = parts_ref[0, :NX].astype(F32)
    for p in range(1, XY):
        total += parts_ref[p, :NX].astype(F32)
    parts = parts_ref[:, NX:, :].astype(F32)
    for z in range(2):
        pieces = [parts[:, (z * 3 + p) * 8 : (z * 3 + p + 1) * 8, :] for p in range(3)]
        lse = jnp.sum(pieces[2], axis=-1, keepdims=True)
        top = jnp.max(lse, axis=0, keepdims=True)
        weight = jnp.exp(lse - top)
        norm = jnp.sum(weight, axis=0)
        out = jnp.concatenate([jnp.sum(p * weight, axis=0) for p in pieces[:2]], axis=1) / norm
        head = with_lse(out, top[0] + jnp.log(norm))
        spare = jnp.concatenate([head[:, 256 : 256 + 128 - BLK], jnp.zeros((24, 128 - BLK), F32)], axis=0)
        turned = total[z * BLK : (z + 1) * BLK].T
        for r in range(4):
            wide = jnp.concatenate([turned[32 * r : 32 * (r + 1)], spare], axis=1)
            both = jnp.concatenate([wide, head[:, :128], head[:, 128:256]], axis=0)
            out_ref[2 * r + z] = both.astype(BF16)


def last_kernel(parts_ref, attention_ref, ffn_ref):
    total = parts_ref[0, :32].astype(F32)
    for p in range(1, 8):
        total += parts_ref[p, :32].astype(F32)
    ffn_ref[...] = total[:, :BLK].astype(BF16)
    role = lax.axis_index("role")
    heads = [parts_ref[2 * role + z].astype(F32) for z in range(2)]
    lse = [jnp.sum(h[:8, BLK:], axis=-1, keepdims=True) for h in heads]
    top = jnp.maximum(lse[0], lse[1])
    weight = [jnp.exp(v - top) for v in lse]
    out = [
        (heads[0][half] * weight[0] + heads[1][half] * weight[1]) / (weight[0] + weight[1])
        for half in (slice(32, 40), slice(40, 48))
    ]
    attention_ref[...] = jnp.concatenate(out, axis=1).astype(BF16)


def shards(queries, cache, beam_sequence, ffn_input, expert_ids, route_weights, gate_up, down_proj):
    shape = jax.ShapeDtypeStruct
    swap = [(0, 1), (1, 0)]

    message = call(
        prep_kernel,
        shape((8, 32, 128), BF16),
        (ffn_input, expert_ids.T, route_weights.T),
        [HBM] * 3,
        FULL,
        scratch=[
            pltpu.VMEM((32, BLK), BF16),
            pltpu.VMEM((3, 32), jnp.int32),
            pltpu.VMEM((3, 32), F32),
            pltpu.VMEM((128, 128), F32),
            pltpu.SemaphoreType.DMA((3,)),
        ],
    )
    rows = lax.all_to_all(message, ("role", "zhi"), 0, 0, tiled=True)
    packed, weight = call(pack_kernel, [shape((XY, NX, 128), BF16), shape((8, 128), F32)], (rows,))
    gathered = lax.all_to_all(packed, ("x", "y"), 0, 0, tiled=True)

    query = queries.reshape(8, 32, 2, 256).transpose(1, 2, 0, 3)
    gate = gate_up.transpose(0, 2, 3, 1)
    units = gate_up.shape[3]
    pairs = [w for a in (cache, gate, down_proj) for w in (a, lax.ppermute(a, "core", swap))]
    attended, gate_c, down_c = call(
        local_kernel,
        [
            shape((32, 8, 384), BF16),
            shape((2, 4 * units, 32 * BLK), BF16),
            shape((2, 2 * units, 32 * BLK), BF16),
        ],
        (beam_sequence, query, *pairs, packed),
        [SMEM] + [HBM] * 7 + [ANY],
        FULL,
        [
            pltpu.VMEM((32, 8, 256), BF16),
            pltpu.VMEM((2,) + cache.shape, BF16),
            pltpu.VMEM((12, units, 64 * BLK), BF16),
            pltpu.VMEM((2, 4 * units, 32 * BLK), BF16),
            pltpu.SemaphoreType.DMA((17,)),
            pltpu.SemaphoreType.DMA((12,)),
            pltpu.SemaphoreType.DMA((8,)),
        ],
        pl.CostEstimate(flops=1 << 31, bytes_accessed=24 << 20, transcendentals=1 << 19),
        [VMEM, HBM, VMEM],
    )

    first, send = call(
        up_kernel,
        [shape((2, 4 * units, ROWS), F32), shape((2, 4 * units, ROWS), BF16)],
        (gathered, gate_c),
    )
    half = call(
        down_kernel,
        shape((XY, NX + NA, 128), BF16),
        (first, lax.ppermute(send, "core", swap), weight, down_c, attended),
    )
    spread = lax.all_to_all(half, ("x", "y"), 0, 0, tiled=True)
    partial = call(turn_kernel, shape((8, 48, 128), BF16), (spread,))
    ends = lax.all_to_all(partial, ("role", "zhi"), 0, 0, tiled=True)
    attention_out, ffn_out = call(
        last_kernel, [shape((8, 256), BF16), shape((32, BLK), BF16)], (ends,)
    )
    return (attention_out, ffn_out)


def solution(mesh):
    fine = Mesh(mesh.devices.reshape(4, 2, 4, 4, 2), ("role", "zhi", "x", "y", "core"))
    tp = ("zhi", "x", "y", "core")
    return jax.shard_map(
        shards,
        mesh=fine,
        in_specs=(
            P("role", None),
            P("role", tp, None),
            P("role"),
            P("role", tp),
            P("role", None),
            P("role", None),
            P("role", None, None, tp),
            P("role", tp, None),
        ),
        out_specs=(P("role", tp), P("role", tp)),
        check_vma=False,
    )
```

```python
import jax
import jax.numpy as jnp
from jax import lax
from jax.experimental import pallas as pl
from jax.experimental.pallas import tpu as pltpu
from jax.sharding import Mesh
from jax.sharding import PartitionSpec as P

F32, BF16 = jnp.float32, jnp.bfloat16
VMEM = pl.BlockSpec(memory_space=pltpu.VMEM)
SMEM = pl.BlockSpec(memory_space=pltpu.SMEM)
ANY = pl.BlockSpec(memory_space=pl.ANY)
HBM = pl.BlockSpec(memory_space=pltpu.HBM)
FULL = 62 << 20
XY = 16
BLK = 112
ROWS = 128
NX = 2 * BLK
NA = 48


def call(kernel, out_shape, args, specs=None, limit=16 << 20, scratch=(), cost=None, outs=None):
    many = isinstance(out_shape, (list, tuple))
    return pl.pallas_call(
        kernel,
        out_shape=out_shape,
        in_specs=specs or [VMEM] * len(args),
        out_specs=outs or ([VMEM] * len(out_shape) if many else VMEM),
        scratch_shapes=scratch,
        cost_estimate=cost,
        compiler_params=pltpu.CompilerParams(vmem_limit_bytes=limit),
    )(*args)


def split3(v):
    hi = v.astype(BF16).astype(F32)
    mid = (v - hi).astype(BF16).astype(F32)
    return hi, mid, (v - hi) - mid


def with_lse(out, lse):
    hi, mid, lo = split3(lse)
    lane = lax.broadcasted_iota(jnp.int32, (out.shape[0], 128), 1)
    tail = jnp.where(lane == 0, hi, jnp.where(lane == 1, mid, jnp.where(lane == 2, lo, 0.0)))
    return jnp.concatenate([out, tail], axis=1)


def lse_of(part):
    return jnp.sum(part[..., 256:], axis=-1, keepdims=True)


def prep_kernel(x_hbm, ids_hbm, route_hbm, out_ref, rows_ref, ids_ref, route_ref, turn_ref, sems):
    copies = [
        pltpu.make_async_copy(src, dst, sems.at[i])
        for i, (src, dst) in enumerate(((ids_hbm, ids_ref), (route_hbm, route_ref), (x_hbm, rows_ref)))
    ]
    for copy in copies:
        copy.start()
    turn_ref[...] = jnp.zeros_like(turn_ref)
    expert = lax.broadcasted_iota(jnp.int32, (8, 32), 0)
    weight = jnp.zeros((8, 32), F32)
    copies[0].wait()
    copies[1].wait()
    for k in range(3):
        weight += jnp.where(ids_ref[k : k + 1, :] == expert, route_ref[k : k + 1, :], 0.0)
    high = weight.astype(BF16).astype(F32)
    turn_ref[BLK : BLK + 8, :32] = high
    turn_ref[BLK + 8 :, :32] = weight - high
    turned = turn_ref[...].T[:32]
    copies[2].wait()
    wide = jnp.concatenate([rows_ref[...].astype(F32), jnp.zeros((32, 128 - BLK), F32)], axis=1)
    message = (wide + turned).astype(BF16)
    for p in range(8):
        out_ref[p] = message


def pack_kernel(rows_ref, out_ref, weight_ref):
    for z in range(2):
        block = jnp.concatenate([rows_ref[2 * r + z] for r in range(4)], axis=0)
        turned = block.astype(F32).T
        if z == 0:
            weight_ref[...] = turned[BLK : BLK + 8] + turned[BLK + 8 :]
        features = turned[:BLK].astype(BF16)
        for p in range(XY):
            out_ref[p, z * BLK : (z + 1) * BLK, :] = features


def attend(seq_ref, queries, caches, waits, out_ref):
    steps = len(queries)
    rows = queries[0].shape[0]
    place = lax.broadcasted_iota(jnp.int32, (rows, 1), 0) % 8
    pick = jnp.zeros((rows, 1), jnp.int32)
    for r in range(8):
        pick = jnp.where(place == r, seq_ref[r], pick)
    second = pick == 1
    dims = (((1,), (1,)), ((), ()))
    scores = [[] for _ in range(steps)]
    for k in range(2):
        waits[k]()
        for step in range(steps):
            both = [
                lax.dot_general(
                    queries[step], caches[k, s, :, :256], dims, preferred_element_type=F32
                )
                for s in range(2)
            ]
            scores[step].append(jnp.where(second, both[1], both[0]) * (256 ** -0.5))
    for step in range(steps):
        top = jnp.maximum(*(jnp.max(v, axis=1, keepdims=True) for v in scores[step]))
        total, summed = 0.0, 0.0
        for k in range(2):
            expo = jnp.exp(scores[step][k] - top)
            total += jnp.sum(expo, axis=1, keepdims=True)
            for s in range(2):
                part = jnp.where(second == (s == 1), expo, 0.0).astype(BF16)
                summed += jnp.dot(part, caches[k, s, :, 256:], preferred_element_type=F32)
        both = with_lse(summed / total, top + jnp.log(total)).reshape(rows // 8, 8, 384)
        out_ref[step * (rows // 8) : (step + 1) * (rows // 8)] = both.astype(BF16)


def local_kernel(
    seq_ref, q_hbm, mine_hbm, theirs_hbm, gate_hbm, got_gate_hbm, down_hbm, got_down_hbm, after_ref,
    attended_ref, out_g_hbm, out_d_hbm,
    q_ref, cache_ref, in_ref, out_g_ref, out_d_ref, cache_sems, in_sems, out_sems,
):
    core = lax.axis_index("core")
    units = in_ref.shape[1]
    positions = cache_ref.shape[2] // 4
    q_load = pltpu.make_async_copy(q_hbm.at[:, core], q_ref, cache_sems.at[16])
    q_load.start()
    cache_loads = []
    for k, ref in enumerate((mine_hbm, theirs_hbm)):
        for s in range(2):
            for i in range(4):
                at = (s, pl.ds(i * positions, positions))
                cache_loads.append(
                    pltpu.make_async_copy(
                        ref.at[at], cache_ref.at[(k,) + at], cache_sems.at[len(cache_loads)]
                    )
                )
                cache_loads[-1].start()
    sources = [ref.at[e, g] for ref in (gate_hbm, got_gate_hbm) for e in range(2) for g in range(2)]
    sources += [ref.at[e] for ref in (down_hbm, got_down_hbm) for e in range(2)]
    loads = [
        pltpu.make_async_copy(source, in_ref.at[i], in_sems.at[i]) for i, source in enumerate(sources)
    ]

    def wait(k):
        for load in cache_loads[8 * k : 8 * k + 8]:
            load.wait()
        for load in loads[:4] if k == 0 else loads[4:]:
            load.start()

    q_load.wait()
    queries = [
        q_ref[step * 16 : (step + 1) * 16].astype(F32).reshape(128, 256).astype(BF16)
        for step in range(2)
    ]
    attend(seq_ref, queries, cache_ref, [lambda: wait(0), lambda: wait(1)], attended_ref)

    stores = []
    for i in range(12):
        at = pl.ds((i if i < 8 else i - 8) * units, units)
        src, dst = (out_g_ref, out_g_hbm) if i < 8 else (out_d_ref, out_d_hbm)
        stores.append(pltpu.make_async_copy(src.at[at], dst.at[at], out_sems.at[i]))
    lane = lax.broadcasted_iota(jnp.int32, (units, 8 * BLK), 1)
    even = ((lane // BLK) % 2 == 0).astype(F32).astype(BF16) > 0

    def sort(i):
        loads[i].wait()
        out = out_g_ref if i < 8 else out_d_ref
        row = (i if i < 8 else i - 8) * units
        for parity in range(2):

            @pl.when(core == parity)
            def _():
                for piece in range(4):
                    low, high = (
                        in_ref[i, :, (z * 4 + piece) * 8 * BLK : (z * 4 + piece + 1) * 8 * BLK]
                        for z in range(2)
                    )
                    if parity:
                        low = jnp.concatenate([low[:, BLK:], low[:, :BLK]], axis=1)
                    else:
                        high = jnp.concatenate([high[:, -BLK:], high[:, :-BLK]], axis=1)
                    to = slice(piece * 8 * BLK, (piece + 1) * 8 * BLK)
                    out[row : row + units, to] = jnp.where(even, low, high)

        stores[i].start()

    for i in range(len(loads)):
        sort(i)
    for store in stores:
        store.wait()


def up_kernel(rows_ref, gate_ref, out_ref, send_ref):
    rows = rows_ref[...].reshape(XY * NX, ROWS)
    both = jnp.dot(gate_ref[...], rows, preferred_element_type=F32)
    out_ref[...] = both
    send_ref[...] = both.astype(BF16)


def activate(both, weight_ref, role, units):
    hidden = []
    for e in range(2):
        gate = both[2 * e * units : (2 * e + 1) * units]
        upper = both[(2 * e + 1) * units : (2 * e + 2) * units]
        weight = weight_ref[pl.ds(2 * role + e, 1), :]
        hidden.append(((gate / (1.0 + jnp.exp(-gate))) * upper * weight).astype(BF16))
    return jnp.concatenate(hidden, axis=0)


def down_kernel(mine_ref, theirs_ref, weight_ref, down_ref, attended_ref, out_ref):
    role = lax.axis_index("role")
    rows = mine_ref.shape[0] // 2
    hidden = jnp.concatenate(
        [
            activate(
                mine_ref[k * rows : (k + 1) * rows]
                + theirs_ref[(1 - k) * rows : (2 - k) * rows].astype(F32),
                weight_ref,
                role,
                rows // 4,
            )
            for k in range(2)
        ],
        axis=0,
    )
    for piece in range(4):
        part = lax.dot_general(
            down_ref[:, piece * 8 * BLK : (piece + 1) * 8 * BLK],
            hidden,
            (((0,), (0,)), ((), ())),
            preferred_element_type=F32,
        )
        out_ref[4 * piece : 4 * piece + 4, :NX, :] = part.astype(BF16).reshape(4, NX, ROWS)
    both = attended_ref[...].astype(F32).reshape(2, XY, 8, 384)
    pieces = [both[z, :, :, p * 128 : (p + 1) * 128] for z in range(2) for p in range(3)]
    out_ref[:, NX:, :] = jnp.concatenate(pieces, axis=1).astype(BF16)


def turn_kernel(parts_ref, out_ref):
    total = parts_ref[0, :NX].astype(F32)
    for p in range(1, XY):
        total += parts_ref[p, :NX].astype(F32)
    parts = parts_ref[:, NX:, :].astype(F32)
    for z in range(2):
        pieces = [parts[:, (z * 3 + p) * 8 : (z * 3 + p + 1) * 8, :] for p in range(3)]
        lse = jnp.sum(pieces[2], axis=-1, keepdims=True)
        top = jnp.max(lse, axis=0, keepdims=True)
        weight = jnp.exp(lse - top)
        norm = jnp.sum(weight, axis=0)
        out = jnp.concatenate([jnp.sum(p * weight, axis=0) for p in pieces[:2]], axis=1) / norm
        head = with_lse(out, top[0] + jnp.log(norm))
        spare = jnp.concatenate([head[:, 256 : 256 + 128 - BLK], jnp.zeros((24, 128 - BLK), F32)], axis=0)
        turned = total[z * BLK : (z + 1) * BLK].T
        for r in range(4):
            wide = jnp.concatenate([turned[32 * r : 32 * (r + 1)], spare], axis=1)
            both = jnp.concatenate([wide, head[:, :128], head[:, 128:256]], axis=0)
            out_ref[2 * r + z] = both.astype(BF16)


def last_kernel(parts_ref, attention_ref, ffn_ref):
    total = parts_ref[0, :32].astype(F32)
    for p in range(1, 8):
        total += parts_ref[p, :32].astype(F32)
    ffn_ref[...] = total[:, :BLK].astype(BF16)
    role = lax.axis_index("role")
    heads = [parts_ref[2 * role + z].astype(F32) for z in range(2)]
    lse = [jnp.sum(h[:8, BLK:], axis=-1, keepdims=True) for h in heads]
    top = jnp.maximum(lse[0], lse[1])
    weight = [jnp.exp(v - top) for v in lse]
    out = [
        (heads[0][half] * weight[0] + heads[1][half] * weight[1]) / (weight[0] + weight[1])
        for half in (slice(32, 40), slice(40, 48))
    ]
    attention_ref[...] = jnp.concatenate(out, axis=1).astype(BF16)


def shards(queries, cache, beam_sequence, ffn_input, expert_ids, route_weights, gate_up, down_proj):
    shape = jax.ShapeDtypeStruct
    swap = [(0, 1), (1, 0)]

    message = call(
        prep_kernel,
        shape((8, 32, 128), BF16),
        (ffn_input, expert_ids.T, route_weights.T),
        [HBM] * 3,
        FULL,
        scratch=[
            pltpu.VMEM((32, BLK), BF16),
            pltpu.VMEM((3, 32), jnp.int32),
            pltpu.VMEM((3, 32), F32),
            pltpu.VMEM((128, 128), F32),
            pltpu.SemaphoreType.DMA((3,)),
        ],
    )
    rows = lax.all_to_all(message, ("role", "zhi"), 0, 0, tiled=True)
    packed, weight = call(pack_kernel, [shape((XY, NX, 128), BF16), shape((8, 128), F32)], (rows,))
    gathered = lax.all_to_all(packed, ("x", "y"), 0, 0, tiled=True)

    query = queries.reshape(8, 32, 2, 256).transpose(1, 2, 0, 3)
    gate = gate_up.transpose(0, 2, 3, 1)
    units = gate_up.shape[3]
    pairs = [w for a in (cache, gate, down_proj) for w in (a, lax.ppermute(a, "core", swap))]
    attended, gate_c, down_c = call(
        local_kernel,
        [
            shape((32, 8, 384), BF16),
            shape((8 * units, 32 * BLK), BF16),
            shape((4 * units, 32 * BLK), BF16),
        ],
        (beam_sequence, query, *pairs, packed),
        [SMEM] + [HBM] * 7 + [ANY],
        FULL,
        [
            pltpu.VMEM((32, 8, 256), BF16),
            pltpu.VMEM((2,) + cache.shape, BF16),
            pltpu.VMEM((12, units, 64 * BLK), BF16),
            pltpu.VMEM((8 * units, 32 * BLK), BF16),
            pltpu.VMEM((4 * units, 32 * BLK), BF16),
            pltpu.SemaphoreType.DMA((17,)),
            pltpu.SemaphoreType.DMA((12,)),
            pltpu.SemaphoreType.DMA((12,)),
        ],
        pl.CostEstimate(flops=1 << 31, bytes_accessed=24 << 20, transcendentals=1 << 19),
        [VMEM, HBM, HBM],
    )

    first, send = call(
        up_kernel,
        [shape((8 * units, ROWS), F32), shape((8 * units, ROWS), BF16)],
        (gathered, gate_c),
    )
    half = call(
        down_kernel,
        shape((XY, NX + NA, 128), BF16),
        (first, lax.ppermute(send, "core", swap), weight, down_c, attended),
    )
    spread = lax.all_to_all(half, ("x", "y"), 0, 0, tiled=True)
    partial = call(turn_kernel, shape((8, 48, 128), BF16), (spread,))
    ends = lax.all_to_all(partial, ("role", "zhi"), 0, 0, tiled=True)
    attention_out, ffn_out = call(
        last_kernel, [shape((8, 256), BF16), shape((32, BLK), BF16)], (ends,)
    )
    return (attention_out, ffn_out)


def solution(mesh):
    fine = Mesh(mesh.devices.reshape(4, 2, 4, 4, 2), ("role", "zhi", "x", "y", "core"))
    tp = ("zhi", "x", "y", "core")
    return jax.shard_map(
        shards,
        mesh=fine,
        in_specs=(
            P("role", None),
            P("role", tp, None),
            P("role"),
            P("role", tp),
            P("role", None),
            P("role", None),
            P("role", None, None, tp),
            P("role", tp, None),
        ),
        out_specs=(P("role", tp), P("role", tp)),
        check_vma=False,
    )
```

```python
import jax
import jax.numpy as jnp
from jax import lax
from jax.experimental import pallas as pl
from jax.experimental.pallas import tpu as pltpu
from jax.sharding import Mesh
from jax.sharding import PartitionSpec as P

F32, BF16 = jnp.float32, jnp.bfloat16
VMEM = pl.BlockSpec(memory_space=pltpu.VMEM)
SMEM = pl.BlockSpec(memory_space=pltpu.SMEM)
ANY = pl.BlockSpec(memory_space=pl.ANY)
HBM = pl.BlockSpec(memory_space=pltpu.HBM)
FULL = 62 << 20
XY = 16
BLK = 112
ROWS = 128
NX = 2 * BLK
NA = 40


def call(kernel, out_shape, args, specs=None, limit=16 << 20, scratch=(), cost=None, outs=None):
    many = isinstance(out_shape, (list, tuple))
    return pl.pallas_call(
        kernel,
        out_shape=out_shape,
        in_specs=specs or [VMEM] * len(args),
        out_specs=outs or ([VMEM] * len(out_shape) if many else VMEM),
        scratch_shapes=scratch,
        cost_estimate=cost,
        compiler_params=pltpu.CompilerParams(vmem_limit_bytes=limit),
    )(*args)


def split3(v):
    hi = v.astype(BF16).astype(F32)
    mid = (v - hi).astype(BF16).astype(F32)
    return hi, mid, (v - hi) - mid


def lse_tile(lse, first=0):
    hi, mid, lo = split3(lse)
    lane = lax.broadcasted_iota(jnp.int32, (lse.shape[0], 128), 1) - first
    return jnp.where(lane == 0, hi, jnp.where(lane == 1, mid, jnp.where(lane == 2, lo, 0.0)))


def with_lse(out, lse):
    return jnp.concatenate([out, lse_tile(lse)], axis=1)


def lse_of(part):
    return jnp.sum(part[..., 256:], axis=-1, keepdims=True)


def prep_kernel(x_hbm, ids_hbm, route_hbm, out_ref, rows_ref, ids_ref, route_ref, turn_ref, sems):
    copies = [
        pltpu.make_async_copy(src, dst, sems.at[i])
        for i, (src, dst) in enumerate(((ids_hbm, ids_ref), (route_hbm, route_ref), (x_hbm, rows_ref)))
    ]
    for copy in copies:
        copy.start()
    turn_ref[...] = jnp.zeros_like(turn_ref)
    expert = lax.broadcasted_iota(jnp.int32, (8, 32), 0)
    weight = jnp.zeros((8, 32), F32)
    copies[0].wait()
    copies[1].wait()
    for k in range(3):
        weight += jnp.where(ids_ref[k : k + 1, :] == expert, route_ref[k : k + 1, :], 0.0)
    high = weight.astype(BF16).astype(F32)
    turn_ref[BLK : BLK + 8, :32] = high
    turn_ref[BLK + 8 :, :32] = weight - high
    turned = turn_ref[...].T[:32]
    copies[2].wait()
    wide = jnp.concatenate([rows_ref[...].astype(F32), jnp.zeros((32, 128 - BLK), F32)], axis=1)
    message = (wide + turned).astype(BF16)
    for p in range(8):
        out_ref[p] = message


def pack_kernel(rows_ref, out_ref, weight_ref):
    for z in range(2):
        block = jnp.concatenate([rows_ref[2 * r + z] for r in range(4)], axis=0)
        turned = block.astype(F32).T
        if z == 0:
            weight_ref[...] = turned[BLK : BLK + 8] + turned[BLK + 8 :]
        features = turned[:BLK].astype(BF16)
        for p in range(XY):
            out_ref[p, z * BLK : (z + 1) * BLK, :] = features


def attend(seq_ref, q_ref, cache, outs):
    core = lax.axis_index("core")
    chunk = 16
    rows = chunk * 8
    place = lax.broadcasted_iota(jnp.int32, (rows, 1), 0) % 8
    pick = jnp.zeros((rows, 1), jnp.int32)
    for r in range(8):
        pick = jnp.where(place == r, seq_ref[r], pick)
    second = pick == 1
    dims = (((1,), (1,)), ((), ()))
    for side, out_ref in enumerate(outs):
        for step in range(q_ref.shape[0] // chunk):
            at = slice(step * chunk, (step + 1) * chunk)
            query = q_ref[at, core if side == 0 else 1 - core]
            query = query.astype(F32).reshape(rows, 256).astype(BF16)
            both = [
                lax.dot_general(query, cache[s, :, :256], dims, preferred_element_type=F32)
                for s in range(2)
            ]
            scores = jnp.where(second, both[1], both[0]) * (256 ** -0.5)
            top = jnp.max(scores, axis=1, keepdims=True)
            expo = jnp.exp(scores - top)
            total = jnp.sum(expo, axis=1, keepdims=True)
            summed = 0.0
            for s in range(2):
                part = jnp.where(second == (s == 1), expo, 0.0).astype(BF16)
                summed += jnp.dot(part, cache[s, :, 256:], preferred_element_type=F32)
            both = with_lse(summed / total, top + jnp.log(total)).reshape(chunk, 8, 384)
            out_ref[at] = both.astype(BF16)


def pair(first, second):
    lse_a, lse_b = lse_of(first), lse_of(second)
    top = jnp.maximum(lse_a, lse_b)
    wa, wb = jnp.exp(lse_a - top), jnp.exp(lse_b - top)
    total = wa + wb
    out = (first[..., :256] * wa + second[..., :256] * wb) / total
    return out, top + jnp.log(total)


def local_kernel(
    seq_ref, q_hbm, cache_hbm, gate_hbm, got_gate_hbm, down_hbm, got_down_hbm, after_ref,
    keep_ref, give_ref, out_g_hbm, out_d_hbm,
    q_ref, cache_ref, in_ref, out_g_ref, out_d_ref, cache_sems, in_sems, out_sems,
):
    core = lax.axis_index("core")
    units = in_ref.shape[1]
    positions = cache_ref.shape[1] // 4
    q_load = pltpu.make_async_copy(q_hbm, q_ref, cache_sems.at[8])
    q_load.start()
    cache_loads = []
    for s in range(2):
        for i in range(4):
            at = (s, pl.ds(i * positions, positions))
            cache_loads.append(
                pltpu.make_async_copy(
                    cache_hbm.at[at], cache_ref.at[at], cache_sems.at[len(cache_loads)]
                )
            )
            cache_loads[-1].start()
    sources = [ref.at[e, g] for ref in (gate_hbm, got_gate_hbm) for e in range(2) for g in range(2)]
    sources += [ref.at[e] for ref in (down_hbm, got_down_hbm) for e in range(2)]
    loads = [
        pltpu.make_async_copy(source, in_ref.at[i], in_sems.at[i]) for i, source in enumerate(sources)
    ]
    for load in loads[:4]:
        load.start()
    q_load.wait()
    for load in cache_loads:
        load.wait()
    for load in loads[4:]:
        load.start()
    attend(seq_ref, q_ref, cache_ref, (keep_ref, give_ref))

    stores = []
    for i in range(12):
        at = pl.ds((i if i < 8 else i - 8) * units, units)
        src, dst = (out_g_ref, out_g_hbm) if i < 8 else (out_d_ref, out_d_hbm)
        stores.append(pltpu.make_async_copy(src.at[at], dst.at[at], out_sems.at[i]))
    lane = lax.broadcasted_iota(jnp.int32, (units, 8 * BLK), 1)
    even = ((lane // BLK) % 2 == 0).astype(F32).astype(BF16) > 0

    def sort(i):
        loads[i].wait()
        out = out_g_ref if i < 8 else out_d_ref
        row = (i if i < 8 else i - 8) * units
        for parity in range(2):

            @pl.when(core == parity)
            def _():
                for piece in range(4):
                    low, high = (
                        in_ref[i, :, (z * 4 + piece) * 8 * BLK : (z * 4 + piece + 1) * 8 * BLK]
                        for z in range(2)
                    )
                    if parity:
                        low = jnp.concatenate([low[:, BLK:], low[:, :BLK]], axis=1)
                    else:
                        high = jnp.concatenate([high[:, -BLK:], high[:, :-BLK]], axis=1)
                    to = slice(piece * 8 * BLK, (piece + 1) * 8 * BLK)
                    out[row : row + units, to] = jnp.where(even, low, high)

        stores[i].start()

    for i in range(len(loads)):
        sort(i)
    for store in stores:
        store.wait()


def up_kernel(rows_ref, gate_ref, out_ref, send_ref):
    rows = rows_ref[...].reshape(XY * NX, ROWS)
    both = jnp.dot(gate_ref[...], rows, preferred_element_type=F32)
    out_ref[...] = both
    send_ref[...] = both.astype(BF16)


def activate(both, weight_ref, role, units):
    hidden = []
    for e in range(2):
        gate = both[2 * e * units : (2 * e + 1) * units]
        upper = both[(2 * e + 1) * units : (2 * e + 2) * units]
        weight = weight_ref[pl.ds(2 * role + e, 1), :]
        hidden.append(((gate / (1.0 + jnp.exp(-gate))) * upper * weight).astype(BF16))
    return jnp.concatenate(hidden, axis=0)


def down_kernel(
    mine_ref, theirs_ref, weight_ref, down_ref, attended_ref, their_attended_ref, out_ref
):
    role = lax.axis_index("role")
    rows = mine_ref.shape[0] // 2
    hidden = jnp.concatenate(
        [
            activate(
                mine_ref[k * rows : (k + 1) * rows]
                + theirs_ref[(1 - k) * rows : (2 - k) * rows].astype(F32),
                weight_ref,
                role,
                rows // 4,
            )
            for k in range(2)
        ],
        axis=0,
    )
    for piece in range(4):
        part = lax.dot_general(
            down_ref[:, piece * 8 * BLK : (piece + 1) * 8 * BLK],
            hidden,
            (((0,), (0,)), ((), ())),
            preferred_element_type=F32,
        )
        out_ref[4 * piece : 4 * piece + 4, :NX, :] = part.astype(BF16).reshape(4, NX, ROWS)
    out, lse = pair(
        attended_ref[...].astype(F32).reshape(256, 384),
        their_attended_ref[...].astype(F32).reshape(256, 384),
    )
    half = XY * 8
    pieces = [
        out[z * half : (z + 1) * half, p * 128 : (p + 1) * 128] for z in range(2) for p in range(2)
    ]
    pieces.append(lse_tile(lse[:half]) + lse_tile(lse[half:], 3))
    pieces = [piece.reshape(XY, 8, 128) for piece in pieces]
    out_ref[:, NX:, :] = jnp.concatenate(pieces, axis=1).astype(BF16)


def turn_kernel(parts_ref, out_ref):
    total = parts_ref[0, :NX].astype(F32)
    for p in range(1, XY):
        total += parts_ref[p, :NX].astype(F32)
    parts = parts_ref[:, NX:, :].astype(F32)
    for z in range(2):
        pieces = [parts[:, (z * 2 + p) * 8 : (z * 2 + p + 1) * 8, :] for p in range(2)]
        lse = jnp.sum(parts[:, 32:, 3 * z : 3 * z + 3], axis=-1, keepdims=True)
        top = jnp.max(lse, axis=0, keepdims=True)
        weight = jnp.exp(lse - top)
        norm = jnp.sum(weight, axis=0)
        out = jnp.concatenate([jnp.sum(p * weight, axis=0) for p in pieces], axis=1) / norm
        head = with_lse(out, top[0] + jnp.log(norm))
        spare = jnp.concatenate([head[:, 256 : 256 + 128 - BLK], jnp.zeros((24, 128 - BLK), F32)], axis=0)
        turned = total[z * BLK : (z + 1) * BLK].T
        for r in range(4):
            wide = jnp.concatenate([turned[32 * r : 32 * (r + 1)], spare], axis=1)
            both = jnp.concatenate([wide, head[:, :128], head[:, 128:256]], axis=0)
            out_ref[2 * r + z] = both.astype(BF16)


def last_kernel(parts_ref, attention_ref, ffn_ref):
    total = parts_ref[0, :32].astype(F32)
    for p in range(1, 8):
        total += parts_ref[p, :32].astype(F32)
    ffn_ref[...] = total[:, :BLK].astype(BF16)
    role = lax.axis_index("role")
    heads = [parts_ref[2 * role + z].astype(F32) for z in range(2)]
    lse = [jnp.sum(h[:8, BLK:], axis=-1, keepdims=True) for h in heads]
    top = jnp.maximum(lse[0], lse[1])
    weight = [jnp.exp(v - top) for v in lse]
    out = [
        (heads[0][half] * weight[0] + heads[1][half] * weight[1]) / (weight[0] + weight[1])
        for half in (slice(32, 40), slice(40, 48))
    ]
    attention_ref[...] = jnp.concatenate(out, axis=1).astype(BF16)


def shards(queries, cache, beam_sequence, ffn_input, expert_ids, route_weights, gate_up, down_proj):
    shape = jax.ShapeDtypeStruct
    swap = [(0, 1), (1, 0)]

    message = call(
        prep_kernel,
        shape((8, 32, 128), BF16),
        (ffn_input, expert_ids.T, route_weights.T),
        [HBM] * 3,
        FULL,
        scratch=[
            pltpu.VMEM((32, BLK), BF16),
            pltpu.VMEM((3, 32), jnp.int32),
            pltpu.VMEM((3, 32), F32),
            pltpu.VMEM((128, 128), F32),
            pltpu.SemaphoreType.DMA((3,)),
        ],
    )
    rows = lax.all_to_all(message, ("role", "zhi"), 0, 0, tiled=True)
    packed, weight = call(pack_kernel, [shape((XY, NX, 128), BF16), shape((8, 128), F32)], (rows,))
    gathered = lax.all_to_all(packed, ("x", "y"), 0, 0, tiled=True)

    query = queries.reshape(8, 32, 2, 256).transpose(1, 2, 0, 3)
    gate = gate_up.transpose(0, 2, 3, 1)
    units = gate_up.shape[3]
    pairs = [w for a in (gate, down_proj) for w in (a, lax.ppermute(a, "core", swap))]
    attended, give, gate_c, down_c = call(
        local_kernel,
        [
            shape((32, 8, 384), BF16),
            shape((32, 8, 384), BF16),
            shape((8 * units, 32 * BLK), BF16),
            shape((4 * units, 32 * BLK), BF16),
        ],
        (beam_sequence, query, cache, *pairs, packed),
        [SMEM] + [HBM] * 6 + [ANY],
        FULL,
        [
            pltpu.VMEM((32, 2, 8, 256), BF16),
            pltpu.VMEM(cache.shape, BF16),
            pltpu.VMEM((12, units, 64 * BLK), BF16),
            pltpu.VMEM((8 * units, 32 * BLK), BF16),
            pltpu.VMEM((4 * units, 32 * BLK), BF16),
            pltpu.SemaphoreType.DMA((9,)),
            pltpu.SemaphoreType.DMA((12,)),
            pltpu.SemaphoreType.DMA((12,)),
        ],
        pl.CostEstimate(flops=1 << 31, bytes_accessed=24 << 20, transcendentals=1 << 19),
        [VMEM, VMEM, HBM, HBM],
    )

    first, send = call(
        up_kernel,
        [shape((8 * units, ROWS), F32), shape((8 * units, ROWS), BF16)],
        (gathered, gate_c),
    )
    half = call(
        down_kernel,
        shape((XY, NX + NA, 128), BF16),
        (first, lax.ppermute(send, "core", swap), weight, down_c, attended, lax.ppermute(give, "core", swap)),
    )
    spread = lax.all_to_all(half, ("x", "y"), 0, 0, tiled=True)
    partial = call(turn_kernel, shape((8, 48, 128), BF16), (spread,))
    ends = lax.all_to_all(partial, ("role", "zhi"), 0, 0, tiled=True)
    attention_out, ffn_out = call(
        last_kernel, [shape((8, 256), BF16), shape((32, BLK), BF16)], (ends,)
    )
    return (attention_out, ffn_out)


def solution(mesh):
    fine = Mesh(mesh.devices.reshape(4, 2, 4, 4, 2), ("role", "zhi", "x", "y", "core"))
    tp = ("zhi", "x", "y", "core")
    return jax.shard_map(
        shards,
        mesh=fine,
        in_specs=(
            P("role", None),
            P("role", tp, None),
            P("role"),
            P("role", tp),
            P("role", None),
            P("role", None),
            P("role", None, None, tp),
            P("role", tp, None),
        ),
        out_specs=(P("role", tp), P("role", tp)),
        check_vma=False,
    )
```

```python
import jax
import jax.numpy as jnp
from jax import lax
from jax.experimental import pallas as pl
from jax.experimental.pallas import tpu as pltpu
from jax.sharding import Mesh
from jax.sharding import PartitionSpec as P

F32, BF16 = jnp.float32, jnp.bfloat16
VMEM = pl.BlockSpec(memory_space=pltpu.VMEM)
SMEM = pl.BlockSpec(memory_space=pltpu.SMEM)
ANY = pl.BlockSpec(memory_space=pl.ANY)
HBM = pl.BlockSpec(memory_space=pltpu.HBM)
FULL = 62 << 20
XY = 16
BLK = 112
ROWS = 128
NX = 2 * BLK
NA = 40


def call(kernel, out_shape, args, specs=None, limit=16 << 20, scratch=(), cost=None, outs=None):
    many = isinstance(out_shape, (list, tuple))
    return pl.pallas_call(
        kernel,
        out_shape=out_shape,
        in_specs=specs or [VMEM] * len(args),
        out_specs=outs or ([VMEM] * len(out_shape) if many else VMEM),
        scratch_shapes=scratch,
        cost_estimate=cost,
        compiler_params=pltpu.CompilerParams(vmem_limit_bytes=limit),
    )(*args)


def split3(v):
    hi = v.astype(BF16).astype(F32)
    mid = (v - hi).astype(BF16).astype(F32)
    return hi, mid, (v - hi) - mid


def lse_tile(lse, first=0):
    hi, mid, lo = split3(lse)
    lane = lax.broadcasted_iota(jnp.int32, (lse.shape[0], 128), 1) - first
    return jnp.where(lane == 0, hi, jnp.where(lane == 1, mid, jnp.where(lane == 2, lo, 0.0)))


def with_lse(out, lse):
    return jnp.concatenate([out, lse_tile(lse)], axis=1)


def lse_of(part):
    return jnp.sum(part[..., 256:], axis=-1, keepdims=True)


def prep_kernel(x_hbm, ids_hbm, route_hbm, out_ref, rows_ref, ids_ref, route_ref, turn_ref, sems):
    copies = [
        pltpu.make_async_copy(src, dst, sems.at[i])
        for i, (src, dst) in enumerate(((ids_hbm, ids_ref), (route_hbm, route_ref), (x_hbm, rows_ref)))
    ]
    for copy in copies:
        copy.start()
    turn_ref[...] = jnp.zeros_like(turn_ref)
    expert = lax.broadcasted_iota(jnp.int32, (8, 32), 0)
    weight = jnp.zeros((8, 32), F32)
    copies[0].wait()
    copies[1].wait()
    for k in range(3):
        weight += jnp.where(ids_ref[k : k + 1, :] == expert, route_ref[k : k + 1, :], 0.0)
    high = weight.astype(BF16).astype(F32)
    turn_ref[BLK : BLK + 8, :32] = high
    turn_ref[BLK + 8 :, :32] = weight - high
    turned = turn_ref[...].T[:32]
    copies[2].wait()
    wide = jnp.concatenate([rows_ref[...].astype(F32), jnp.zeros((32, 128 - BLK), F32)], axis=1)
    message = (wide + turned).astype(BF16)
    for p in range(8):
        out_ref[p] = message


def pack_kernel(rows_ref, out_ref, weight_ref):
    for z in range(2):
        block = jnp.concatenate([rows_ref[2 * r + z] for r in range(4)], axis=0)
        turned = block.astype(F32).T
        if z == 0:
            weight_ref[...] = turned[BLK : BLK + 8] + turned[BLK + 8 :]
        features = turned[:BLK].astype(BF16)
        for p in range(XY):
            out_ref[p, z * BLK : (z + 1) * BLK, :] = features


def attend(seq_ref, q_ref, cache, outs):
    core = lax.axis_index("core")
    chunk = 16
    rows = chunk * 8
    place = lax.broadcasted_iota(jnp.int32, (rows, 1), 0) % 8
    pick = jnp.zeros((rows, 1), jnp.int32)
    for r in range(8):
        pick = jnp.where(place == r, seq_ref[r], pick)
    second = pick == 1
    dims = (((1,), (1,)), ((), ()))
    for side, out_ref in enumerate(outs):
        for step in range(q_ref.shape[0] // chunk):
            at = slice(step * chunk, (step + 1) * chunk)
            query = q_ref[at, core if side == 0 else 1 - core]
            query = query.astype(F32).reshape(rows, 256).astype(BF16)
            both = [
                lax.dot_general(query, cache[s, :, :256], dims, preferred_element_type=F32)
                for s in range(2)
            ]
            scores = jnp.where(second, both[1], both[0]) * (256 ** -0.5)
            top = jnp.max(scores, axis=1, keepdims=True)
            expo = jnp.exp(scores - top)
            total = jnp.sum(expo, axis=1, keepdims=True)
            summed = 0.0
            for s in range(2):
                part = jnp.where(second == (s == 1), expo, 0.0).astype(BF16)
                summed += jnp.dot(part, cache[s, :, 256:], preferred_element_type=F32)
            both = with_lse(summed / total, top + jnp.log(total)).reshape(chunk, 8, 384)
            out_ref[at] = both.astype(BF16)


def pair(first, second):
    lse_a, lse_b = lse_of(first), lse_of(second)
    top = jnp.maximum(lse_a, lse_b)
    wa, wb = jnp.exp(lse_a - top), jnp.exp(lse_b - top)
    total = wa + wb
    out = (first[..., :256] * wa + second[..., :256] * wb) / total
    return out, top + jnp.log(total)


def local_kernel(
    seq_ref, q_hbm, cache_hbm, gate_hbm, got_gate_hbm, down_hbm, got_down_hbm, after_ref,
    keep_ref, give_ref, out_g_hbm, out_d_hbm,
    q_ref, cache_ref, in_ref, out_g_ref, out_d_ref, cache_sems, in_sems, out_sems,
):
    core = lax.axis_index("core")
    units = in_ref.shape[1]
    positions = cache_ref.shape[1] // 4
    q_load = pltpu.make_async_copy(q_hbm, q_ref, cache_sems.at[8])
    q_load.start()
    cache_loads = []
    for s in range(2):
        for i in range(4):
            at = (s, pl.ds(i * positions, positions))
            cache_loads.append(
                pltpu.make_async_copy(
                    cache_hbm.at[at], cache_ref.at[at], cache_sems.at[len(cache_loads)]
                )
            )
            cache_loads[-1].start()
    sources = [ref.at[e, g] for ref in (gate_hbm, got_gate_hbm) for e in range(2) for g in range(2)]
    sources += [ref.at[e] for ref in (down_hbm, got_down_hbm) for e in range(2)]
    loads = [
        pltpu.make_async_copy(source, in_ref.at[i], in_sems.at[i]) for i, source in enumerate(sources)
    ]
    q_load.wait()
    for load in loads[:4]:
        load.start()
    for load in cache_loads:
        load.wait()
    for load in loads[4:]:
        load.start()
    attend(seq_ref, q_ref, cache_ref, (keep_ref, give_ref))

    stores = []
    for i in range(12):
        at = pl.ds((i if i < 8 else i - 8) * units, units)
        src, dst = (out_g_ref, out_g_hbm) if i < 8 else (out_d_ref, out_d_hbm)
        stores.append(pltpu.make_async_copy(src.at[at], dst.at[at], out_sems.at[i]))
    lane = lax.broadcasted_iota(jnp.int32, (units, 8 * BLK), 1)
    even = ((lane // BLK) % 2 == 0).astype(F32).astype(BF16) > 0

    def sort(i):
        loads[i].wait()
        out = out_g_ref if i < 8 else out_d_ref
        row = (i if i < 8 else i - 8) * units
        for parity in range(2):

            @pl.when(core == parity)
            def _():
                for piece in range(4):
                    low, high = (
                        in_ref[i, :, (z * 4 + piece) * 8 * BLK : (z * 4 + piece + 1) * 8 * BLK]
                        for z in range(2)
                    )
                    if parity:
                        low = jnp.concatenate([low[:, BLK:], low[:, :BLK]], axis=1)
                    else:
                        high = jnp.concatenate([high[:, -BLK:], high[:, :-BLK]], axis=1)
                    to = slice(piece * 8 * BLK, (piece + 1) * 8 * BLK)
                    out[row : row + units, to] = jnp.where(even, low, high)

        stores[i].start()

    for i in range(len(loads)):
        sort(i)
    for store in stores:
        store.wait()


def up_kernel(rows_ref, gate_ref, out_ref, send_ref):
    rows = rows_ref[...].reshape(XY * NX, ROWS)
    both = jnp.dot(gate_ref[...], rows, preferred_element_type=F32)
    out_ref[...] = both
    send_ref[...] = both.astype(BF16)


def activate(both, weight_ref, role, units):
    hidden = []
    for e in range(2):
        gate = both[2 * e * units : (2 * e + 1) * units]
        upper = both[(2 * e + 1) * units : (2 * e + 2) * units]
        weight = weight_ref[pl.ds(2 * role + e, 1), :]
        hidden.append(((gate / (1.0 + jnp.exp(-gate))) * upper * weight).astype(BF16))
    return jnp.concatenate(hidden, axis=0)


def down_kernel(
    mine_ref, theirs_ref, weight_ref, down_ref, attended_ref, their_attended_ref, out_ref
):
    role = lax.axis_index("role")
    rows = mine_ref.shape[0] // 2
    hidden = jnp.concatenate(
        [
            activate(
                mine_ref[k * rows : (k + 1) * rows]
                + theirs_ref[(1 - k) * rows : (2 - k) * rows].astype(F32),
                weight_ref,
                role,
                rows // 4,
            )
            for k in range(2)
        ],
        axis=0,
    )
    for piece in range(4):
        part = lax.dot_general(
            down_ref[:, piece * 8 * BLK : (piece + 1) * 8 * BLK],
            hidden,
            (((0,), (0,)), ((), ())),
            preferred_element_type=F32,
        )
        out_ref[4 * piece : 4 * piece + 4, :NX, :] = part.astype(BF16).reshape(4, NX, ROWS)
    out, lse = pair(
        attended_ref[...].astype(F32).reshape(256, 384),
        their_attended_ref[...].astype(F32).reshape(256, 384),
    )
    half = XY * 8
    pieces = [
        out[z * half : (z + 1) * half, p * 128 : (p + 1) * 128] for z in range(2) for p in range(2)
    ]
    pieces.append(lse_tile(lse[:half]) + lse_tile(lse[half:], 3))
    pieces = [piece.reshape(XY, 8, 128) for piece in pieces]
    out_ref[:, NX:, :] = jnp.concatenate(pieces, axis=1).astype(BF16)


def turn_kernel(parts_ref, out_ref):
    total = parts_ref[0, :NX].astype(F32)
    for p in range(1, XY):
        total += parts_ref[p, :NX].astype(F32)
    parts = parts_ref[:, NX:, :].astype(F32)
    for z in range(2):
        pieces = [parts[:, (z * 2 + p) * 8 : (z * 2 + p + 1) * 8, :] for p in range(2)]
        lse = jnp.sum(parts[:, 32:, 3 * z : 3 * z + 3], axis=-1, keepdims=True)
        top = jnp.max(lse, axis=0, keepdims=True)
        weight = jnp.exp(lse - top)
        norm = jnp.sum(weight, axis=0)
        out = jnp.concatenate([jnp.sum(p * weight, axis=0) for p in pieces], axis=1) / norm
        head = with_lse(out, top[0] + jnp.log(norm))
        spare = jnp.concatenate([head[:, 256 : 256 + 128 - BLK], jnp.zeros((24, 128 - BLK), F32)], axis=0)
        turned = total[z * BLK : (z + 1) * BLK].T
        for r in range(4):
            wide = jnp.concatenate([turned[32 * r : 32 * (r + 1)], spare], axis=1)
            both = jnp.concatenate([wide, head[:, :128], head[:, 128:256]], axis=0)
            out_ref[2 * r + z] = both.astype(BF16)


def last_kernel(parts_ref, attention_ref, ffn_ref):
    total = parts_ref[0, :32].astype(F32)
    for p in range(1, 8):
        total += parts_ref[p, :32].astype(F32)
    ffn_ref[...] = total[:, :BLK].astype(BF16)
    role = lax.axis_index("role")
    heads = [parts_ref[2 * role + z].astype(F32) for z in range(2)]
    lse = [jnp.sum(h[:8, BLK:], axis=-1, keepdims=True) for h in heads]
    top = jnp.maximum(lse[0], lse[1])
    weight = [jnp.exp(v - top) for v in lse]
    out = [
        (heads[0][half] * weight[0] + heads[1][half] * weight[1]) / (weight[0] + weight[1])
        for half in (slice(32, 40), slice(40, 48))
    ]
    attention_ref[...] = jnp.concatenate(out, axis=1).astype(BF16)


def shards(queries, cache, beam_sequence, ffn_input, expert_ids, route_weights, gate_up, down_proj):
    shape = jax.ShapeDtypeStruct
    swap = [(0, 1), (1, 0)]

    message = call(
        prep_kernel,
        shape((8, 32, 128), BF16),
        (ffn_input, expert_ids.T, route_weights.T),
        [HBM] * 3,
        FULL,
        scratch=[
            pltpu.VMEM((32, BLK), BF16),
            pltpu.VMEM((3, 32), jnp.int32),
            pltpu.VMEM((3, 32), F32),
            pltpu.VMEM((128, 128), F32),
            pltpu.SemaphoreType.DMA((3,)),
        ],
    )
    rows = lax.all_to_all(message, ("role", "zhi"), 0, 0, tiled=True)
    packed, weight = call(pack_kernel, [shape((XY, NX, 128), BF16), shape((8, 128), F32)], (rows,))
    gathered = lax.all_to_all(packed, ("x", "y"), 0, 0, tiled=True)

    query = queries.reshape(8, 32, 2, 256).transpose(1, 2, 0, 3)
    gate = gate_up.transpose(0, 2, 3, 1)
    units = gate_up.shape[3]
    pairs = [w for a in (gate, down_proj) for w in (a, lax.ppermute(a, "core", swap))]
    attended, give, gate_c, down_c = call(
        local_kernel,
        [
            shape((32, 8, 384), BF16),
            shape((32, 8, 384), BF16),
            shape((8 * units, 32 * BLK), BF16),
            shape((4 * units, 32 * BLK), BF16),
        ],
        (beam_sequence, query, cache, *pairs, packed),
        [SMEM] + [HBM] * 6 + [ANY],
        FULL,
        [
            pltpu.VMEM((32, 2, 8, 256), BF16),
            pltpu.VMEM(cache.shape, BF16),
            pltpu.VMEM((12, units, 64 * BLK), BF16),
            pltpu.VMEM((8 * units, 32 * BLK), BF16),
            pltpu.VMEM((4 * units, 32 * BLK), BF16),
            pltpu.SemaphoreType.DMA((9,)),
            pltpu.SemaphoreType.DMA((12,)),
            pltpu.SemaphoreType.DMA((12,)),
        ],
        pl.CostEstimate(flops=1 << 31, bytes_accessed=24 << 20, transcendentals=1 << 19),
        [VMEM, VMEM, HBM, HBM],
    )

    first, send = call(
        up_kernel,
        [shape((8 * units, ROWS), F32), shape((8 * units, ROWS), BF16)],
        (gathered, gate_c),
    )
    half = call(
        down_kernel,
        shape((XY, NX + NA, 128), BF16),
        (first, lax.ppermute(send, "core", swap), weight, down_c, attended, lax.ppermute(give, "core", swap)),
    )
    spread = lax.all_to_all(half, ("x", "y"), 0, 0, tiled=True)
    partial = call(turn_kernel, shape((8, 48, 128), BF16), (spread,))
    ends = lax.all_to_all(partial, ("role", "zhi"), 0, 0, tiled=True)
    attention_out, ffn_out = call(
        last_kernel, [shape((8, 256), BF16), shape((32, BLK), BF16)], (ends,)
    )
    return (attention_out, ffn_out)


def solution(mesh):
    fine = Mesh(mesh.devices.reshape(4, 2, 4, 4, 2), ("role", "zhi", "x", "y", "core"))
    tp = ("zhi", "x", "y", "core")
    return jax.shard_map(
        shards,
        mesh=fine,
        in_specs=(
            P("role", None),
            P("role", tp, None),
            P("role"),
            P("role", tp),
            P("role", None),
            P("role", None),
            P("role", None, None, tp),
            P("role", tp, None),
        ),
        out_specs=(P("role", tp), P("role", tp)),
        check_vma=False,
    )
```
